128 devices in a mesh: dp: 16 (over x, y), mp: 8 (over z, core).
Axes of the slice: x: 4, y: 4, z: 4, core: 2. Of those that a mesh axis runs over, the one named last changes fastest.
Arguments:
- hidden_act: bfloat16 [8192, 14336], P('dp', 'mp'), may hold values from -6 to 6
- cotangent: bfloat16 [8192, 4096], P('dp', 'mp'), may hold values from -6 to 6
- weight: bfloat16 [14336, 4096], P('mp'), may hold values from -0.046875 to 0.046875
- deltas: bfloat16 [512, 16384], P('mp'), may hold values from -0.29882812 to 0.29882812
- block_ids: int32 [512], P('mp'), may hold values from 0 to 447, as said below
- owners: int32 [512, 1], P('mp'), may hold values from 0 to 15; in each aligned block of 64 rows (0 to 63, 64 to 127, ...) at most 8 rows name the same one
- first_moment: float32 [8, 128, 16384], P('mp', 'dp'), may hold values from -6 to 6
- second_moment: float32 [8, 128, 16384], P('mp', 'dp'), may hold values from 0.3 to 3
Outputs:
- input_grad: bfloat16 [8192, 14336], P('dp', 'mp')
- new_deltas: bfloat16 [512, 16384], P('mp')
- new_first: float32 [8, 128, 16384], P('mp', 'dp')
- new_second: float32 [8, 128, 16384], P('mp', 'dp')
The draws below stay inside these ranges and needn't reach their ends.
Inputs may be any that keep to these rules, and one draw needn't show every extreme that they name: `block_ids`: within one index of mp the 64 entries are distinct local block numbers row * 32 + column, with row below 14; the last number is always among them. `owners`: among the 64 blocks of one index of mp no owner is named more than 8 times, a bound that some block reaches.
All inputs are finite; a program needn't handle non-finite values.
Results may differ from the reference program's by a relative error of at most 0.0048.
Values may be sent and summed in bfloat16 or wider, within the bound.
A program may use at most 192 MiB of HBM per device.

```python
import math
import jax
import jax.numpy as jnp
import numpy as np
from jax import lax

D = 4096
FF = 14336
BS = 128
NBL = 64
TOKENS = 8192
CAP = 8
RB = 14
CB = 32
N_DP = 16
N_MP = 8


def draw_block_ids(key, part):
    key = jax.random.fold_in(key, 11)
    limit = FF // BS // N_MP * (D // BS)
    pieces = []
    for shard_number in range(N_MP):
        shard_key = jax.random.fold_in(key, shard_number)
        chosen = jax.random.permutation(shard_key, limit - 1)[:NBL - 1].astype(jnp.int32)
        chosen = jnp.concatenate([chosen, jnp.array([limit - 1], jnp.int32)])
        pieces.append(jax.random.permutation(jax.random.fold_in(shard_key, 1), chosen).astype(jnp.int32))
    return jnp.concatenate(pieces).astype(jnp.int32)


def block_scale(key, shape, cuts, low, largest):
    def one(axis_at, shards_of):
        steps = jax.random.uniform(jax.random.fold_in(jax.random.fold_in(key, 6), axis_at), (shards_of,), jnp.float32, low / len(cuts), largest / len(cuts))
        return jnp.repeat(jnp.exp(steps), shape[axis_at] // shards_of).reshape((-1,) + (1,) * (len(shape) - axis_at - 1))

    gain = one(*cuts[0])
    for cut in cuts[1:]:
        gain = gain * one(*cut)
    return gain


def deal_out(stream_key, own, number, rows, amount, top, most, lean):
    sequence = jax.random.permutation(stream_key, amount)
    crowded, usual = load_shares(amount, rows * top, most, lean, True), load_shares(amount, rows * top, most, lean, False)
    places = jnp.arange(amount)

    def named(sizes, rotation):
        used = int((sizes > 0).sum())
        fixed = max(1, used // 4)
        shifted = fixed + (places - fixed + rotation * (used - fixed)) % max(1, amount - fixed)
        return jnp.zeros((amount,), jnp.int32).at[sequence[jnp.where(places < fixed, places, shifted)]].set(jnp.asarray(sizes, jnp.int32))

    sizes = jnp.where(number % 4 == 0, named(crowded, number // 4), named(usual, number - number // 4 - 1))
    mixed = jax.random.permutation(jax.random.fold_in(own, 3), amount)
    donor, receiver = mixed[0:amount // 2 * 2:2], mixed[1:amount // 2 * 2:2]
    slack = jnp.minimum(sizes[donor] - 1, most - sizes[receiver]) // 2
    slack = jnp.where((donor == sequence[0]) | (receiver == sequence[0]) | (sizes[receiver] == 0), 0, jnp.maximum(slack, 0))
    shifted = jax.random.randint(jax.random.fold_in(own, 4), (amount // 2,), 0, 1 << 20) % (slack + 1)
    sizes = sizes.at[donor].add(-shifted).at[receiver].add(shifted)
    members = jnp.searchsorted(jnp.cumsum(sizes), jnp.arange(rows * top), side="right").astype(jnp.int32)
    listing = members.reshape(top, rows).T
    listing = listing[jax.random.permutation(jax.random.fold_in(own, 1), rows)]
    rotation = jax.random.randint(jax.random.fold_in(own, 2), (rows, 1), 0, top)
    return jnp.take_along_axis(listing, (jnp.arange(top)[None, :] + rotation) % top, axis=1)


def load_shares(amount, total, reach, lean, full):
    loads = [(1 << 20) // math.isqrt(standing ** lean) + 1 for standing in range(1, amount + 1)]
    largest = reach if full else min(reach, max(-(-total // amount), total * loads[0] // sum(loads)))
    least = 1 if total - largest >= amount - 1 else 0
    holding, rest = [largest] + [least] * (amount - 1), total - largest - least * (amount - 1)
    while rest > 0:
        candidates = [i for i in range(1, amount) if holding[i] < largest] or [i for i in range(1, amount) if holding[i] < reach]
        mass, remaining = sum([loads[i] for i in candidates]), rest
        for i in candidates:
            more = min(reach - holding[i], max(1, remaining * loads[i] // mass), rest)
            holding[i] = holding[i] + more
            rest = rest - more
    return np.array(holding)


def noise(stream_key, extent, deviation, most, split=(), held_as=jnp.bfloat16):
    values = deviation * jax.random.normal(stream_key, extent, jnp.float32)
    if split:
        values = values * block_scale(stream_key, extent, split, -0.22, 0.18)
    return jnp.clip(values, -most, most).astype(held_as)


def setup_inputs(seed: int = 0) -> dict:
    streams_of = jax.random.split(jax.random.key(seed), 9)
    hidden_act = noise(streams_of[0], (TOKENS, FF), 1.0, 6.0, ((0, 16), (1, 8)))
    cotangent = noise(streams_of[1], (TOKENS, D), 1.0, 6.0, ((0, 16), (1, 8)))
    weight = noise(streams_of[2], (FF, D), FF ** -0.5, 0.046875, ((0, 8),))
    deltas = noise(streams_of[3], (N_MP * NBL, BS * BS), 0.05, 0.29882812, ((0, 8),))
    block_ids = draw_block_ids(jax.random.fold_in(streams_of[8], 71), 0)
    owners_keys = jax.random.split(jax.random.fold_in(streams_of[5], 1), (N_MP * NBL) // NBL)
    owners_turns = jax.random.permutation(jax.random.fold_in(streams_of[5], 3), (N_MP * NBL) // NBL)
    owners = jax.vmap(lambda own, number: deal_out(jax.random.fold_in(streams_of[5], 2), own, number, NBL, N_DP, 1, CAP, 2))(owners_keys, owners_turns).reshape((N_MP * NBL, 1))
    first_moment = noise(streams_of[6], (N_MP, N_DP * CAP, BS * BS), 1.0, 6.0, ((0, 8), (1, 16)), jnp.float32)
    second_moment = jnp.clip(jnp.exp(math.log(3.0) - 2.3025851 * jax.random.uniform(streams_of[7], (N_MP, N_DP * CAP, BS * BS), jnp.float32) ** block_scale(streams_of[7], (N_MP, N_DP * CAP, BS * BS), ((0, 8), (1, 16)), -0.2, 0.2)), 0.3, 3.0)
    return {"hidden_act": hidden_act, "cotangent": cotangent, "weight": weight, "deltas": deltas, "block_ids": block_ids, "owners": owners, "first_moment": first_moment, "second_moment": second_moment}


BETA_ONE = 0.9
BETA_TWO = 0.95
LEARN_RATE = 0.02
EPSILON = 1e-08
CORRECT_ONE = 1.0 - 0.9 ** 4
CORRECT_TWO = 1.0 - 0.95 ** 4

def reference(hidden_act, cotangent, weight, deltas, block_ids, owners, first_moment, second_moment):
    total_blocks = N_MP * NBL
    shard_of = (jnp.arange(total_blocks) // NBL).astype(jnp.int32)
    block_rows = (shard_of * RB + block_ids // CB).astype(jnp.int32)
    block_cols = (block_ids % CB).astype(jnp.int32)
    tiles = deltas.reshape(total_blocks, BS, BS)
    dense = jnp.zeros((FF // BS, CB, BS, BS), deltas.dtype).at[block_rows, block_cols].set(tiles)
    dense = dense.transpose(0, 2, 1, 3).reshape(FF, D)
    merged = (weight + dense).astype(weight.dtype)
    dims = (((1,), (1,)), ((), ()))
    input_grad = lax.dot_general(cotangent, merged, dims, preferred_element_type=jnp.float32).astype(jnp.bfloat16)

    def one_block(pair):
        row_start = (pair[0] * BS).astype(jnp.int32)
        col_start = (pair[1] * BS).astype(jnp.int32)
        left_tile = lax.dynamic_slice_in_dim(hidden_act, row_start, BS, 1)
        right_tile = lax.dynamic_slice_in_dim(cotangent, col_start, BS, 1)
        return jnp.dot(left_tile.T, right_tile, preferred_element_type=jnp.float32)
    block_grad = lax.map(one_block, (block_rows, block_cols)) / jnp.sqrt(jnp.float32(TOKENS))
    block_grad = block_grad.reshape(N_MP, NBL, BS * BS)
    owner_list = owners[:, 0].reshape(N_MP, NBL)
    positions = jnp.arange(NBL)
    same_owner = owner_list[:, :, None] == owner_list[:, None, :]
    earlier = positions[None, :] < positions[:, None]
    slot_rank = lax.optimization_barrier(jnp.sum(jnp.where(same_owner & earlier[None], 1, 0), axis=2)).astype(jnp.int32)
    target = (owner_list * CAP + slot_rank).astype(jnp.int32)
    shard_index = jnp.arange(N_MP).astype(jnp.int32)[:, None]
    first_prev = first_moment[shard_index, target]
    second_prev = second_moment[shard_index, target]
    first_next = BETA_ONE * first_prev + (1.0 - BETA_ONE) * block_grad
    second_next = BETA_TWO * second_prev + (1.0 - BETA_TWO) * block_grad * block_grad
    current = deltas.astype(jnp.float32).reshape(N_MP, NBL, BS * BS)
    stepped = current - LEARN_RATE * (first_next / CORRECT_ONE) / (jnp.sqrt(second_next / CORRECT_TWO) + EPSILON)
    new_deltas = stepped.astype(jnp.bfloat16).reshape(total_blocks, BS * BS)
    new_first = first_moment.at[shard_index, target].set(first_next)
    new_second = second_moment.at[shard_index, target].set(second_next)
    return (input_grad, new_deltas, new_first, new_second)
```

```python
import functools
import math

import jax
import jax.numpy as jnp
from jax import lax
from jax.experimental import pallas as pl
from jax.experimental.pallas import tpu as pltpu
from jax.sharding import PartitionSpec as P

D = 4096
BS = 128
TOK = 512
FFL = 1792
RB = 14
CB = 32
NBL = 64
CAP = 8
TILES = 7
TILE = FFL // TILES

BETA_ONE = 0.9
BETA_TWO = 0.95
LEARN_RATE = 0.02
EPSILON = 1e-08
CORRECT_ONE = 1.0 - 0.9**4
CORRECT_TWO = 1.0 - 0.95**4
GRAD_SCALE = 1.0 / math.sqrt(8192.0)

MESH = pl.DeviceIdType.MESH
BF16, F32, I32 = jnp.bfloat16, jnp.float32, jnp.int32
N_REMOTE = 64


def mod4(v):
    return lax.rem(v + 4, 4)


def kernel(
    cot, hid, weight, deltas, dblocks, ids_row, own_row, first, second,
    grad_out, deltas_out, first_out, second_out,
    cbuf, hbuf, ht, dense, wbuf, drow, dblk, stage, rx, ry, cb, r1, rx2, ry2, cb2, gsum,
    gath, mbuf, vbuf, mnew, vnew, cur, dnew, obuf, tab, stab, pick,
    lsem, wsem, osem, ssem, rsem,
):
    dp, mp = lax.axis_index("dp"), lax.axis_index("mp")
    xx, yy = dp // 4, lax.rem(dp, 4)
    zz, core = mp // 2, lax.rem(mp, 2)
    x_up, x_dn = (mod4(xx + 1) * 4 + yy, mp), (mod4(xx - 1) * 4 + yy, mp)
    y_up, y_dn = (xx * 4 + mod4(yy + 1), mp), (xx * 4 + mod4(yy - 1), mp)
    z_up, z_dn = (dp, mod4(zz + 1) * 2 + core), (dp, mod4(zz - 1) * 2 + core)
    mate = (dp, zz * 2 + 1 - core)

    def local_copy(src, dst, i):
        c = pltpu.make_async_copy(src, dst, lsem.at[i])
        c.start()
        return c

    def col(z, c, half, width=256):
        return pl.ds(pl.multiple_of((z * 2 + c) * 512 + half * 256, 256), width)

    cp_cot = local_copy(cot, cbuf.at[:, col(zz, core, 0, 512)], 0)
    cp_hid = local_copy(hid, hbuf, 1)
    cp_dr = local_copy(deltas, drow, 2)
    cp_m = local_copy(first, mbuf, 3)
    cp_v = local_copy(second, vbuf, 4)
    cp_db = local_copy(dblocks, dblk.at[pl.ds(0, NBL)], 5)

    def w_copy(n, slot):
        return pltpu.make_async_copy(
            weight.at[pl.ds(pl.multiple_of(n * TILE, TILE), TILE)], wbuf.at[slot], wsem.at[slot])

    w_copy(0, 0).start()

    barrier = pltpu.get_barrier_semaphore()
    for dev in (x_up, x_dn, y_up, y_dn, z_up, z_dn, mate):
        pl.semaphore_signal(barrier, inc=1, device_id=dev, device_id_type=MESH)
    pl.semaphore_wait(barrier, 7)

    sent = []

    def send(src, dst, dev):
        i = len(sent)
        c = pltpu.make_async_remote_copy(
            src_ref=src, dst_ref=dst, send_sem=ssem.at[i], recv_sem=rsem.at[i],
            device_id=dev, device_id_type=MESH)
        c.start()
        sent.append(c)
        return c

    def share(where, dev):
        return send(cbuf.at[:, where], cbuf.at[:, where], dev)

    cp_cot.wait()
    up_a = share(col(zz, core, 0), z_up)
    dn_b = share(col(zz, core, 1), z_dn)
    to_mate = share(col(zz, core, 0, 512), mate)
    up_b = share(col(zz, core, 1), z_up)
    dn_a = share(col(zz, core, 0), z_dn)

    ri = lax.broadcasted_iota(I32, (NBL, NBL), 0)
    ci = lax.broadcasted_iota(I32, (NBL, NBL), 1)
    eye = ri == ci
    owns = jnp.broadcast_to(own_row[...], (NBL, NBL))
    own_col = jnp.sum(jnp.where(eye, owns, 0), axis=1, keepdims=True)
    ids_col = jnp.sum(jnp.where(eye, jnp.broadcast_to(ids_row[...], (NBL, NBL)), 0), axis=1, keepdims=True)
    slot_col = jnp.sum(jnp.where((own_col == owns) & (ci < ri), 1, 0), axis=1, keepdims=True)
    target_col = own_col * CAP + slot_col
    target_row = jnp.sum(jnp.where(eye, jnp.broadcast_to(target_col, (NBL, NBL)), 0), axis=0, keepdims=True)
    block_at = lax.broadcasted_iota(I32, (NBL, 512), 1)
    number = lax.broadcasted_iota(I32, (NBL, 512), 0)
    inverse = NBL - jnp.max(jnp.where(ids_col == block_at, NBL - number, 0), axis=0, keepdims=True)
    place = jnp.max(jnp.where(target_col == block_at, jnp.broadcast_to(ids_col, (NBL, 512)), 0), axis=0, keepdims=True)
    tab[...] = jnp.zeros_like(tab)
    tab[0:1, :] = inverse
    tab[1:2, :] = place
    cp_tab = local_copy(tab, stab, 6)
    mine = lax.broadcasted_iota(I32, (16, NBL), 0)
    hit = jnp.where((target_row == dp * CAP + mine) & (mine < CAP), 1.0, 0.0)
    filled = jnp.sum(hit, axis=1, keepdims=True)[0:CAP] > 0.5
    q = lax.broadcasted_iota(I32, (NBL, 256), 1)
    for h in range(2):
        dev_at = own_col if h else lax.rem(own_col, 4) * 4 + own_col // 4
        for half in range(2):
            pick[h, half] = jnp.where(q == dev_at * 16 + half * 8 + slot_col, 1.0, 0.0).astype(BF16)

    cp_hid.wait()

    @pl.loop(0, TILES)
    def _(i):
        rows = pl.ds(pl.multiple_of(i * TILE, TILE), TILE)
        ht[rows, :] = hbuf[:, rows].T

    def products(z, c, half, width):
        first_col = (z * 2 + c) * 4 + half * 2
        where = col(z, c, half, width)

        @pl.loop(0, TILES)
        def _(i):
            rows = pl.ds(pl.multiple_of(i * TILE, TILE), TILE)
            g = jnp.dot(ht[rows, :], cbuf[:, where], preferred_element_type=F32).astype(BF16)
            for r in range(2):
                for k in range(width // BS):
                    dense[(i * 2 + r) * CB + first_col + k] = g[r * BS:(r + 1) * BS, k * BS:(k + 1) * BS]

    mate_core = 1 - core
    zu, zd, zo = mod4(zz + 1), mod4(zz - 1), mod4(zz + 2)
    products(zz, core, 0, 512)
    to_mate.wait_recv()
    products(zz, mate_core, 0, 512)
    up_a.wait_recv()
    fw_a = share(col(zd, core, 0), z_up)
    m_da = share(col(zd, core, 0), mate)
    dn_b.wait_recv()
    fw_b = share(col(zu, core, 1), z_dn)
    m_ub = share(col(zu, core, 1), mate)
    products(zd, core, 0, 256)
    products(zu, core, 1, 256)
    m_da.wait_recv()
    products(zd, mate_core, 0, 256)
    m_ub.wait_recv()
    products(zu, mate_core, 1, 256)
    up_b.wait_recv()
    m_db = share(col(zd, core, 1), mate)
    dn_a.wait_recv()
    m_ua = share(col(zu, core, 0), mate)
    products(zd, core, 1, 256)
    products(zu, core, 0, 256)
    m_db.wait_recv()
    products(zd, mate_core, 1, 256)
    m_ua.wait_recv()
    products(zu, mate_core, 0, 256)
    fw_a.wait_recv()
    m_oa = share(col(zo, core, 0), mate)
    fw_b.wait_recv()
    m_ob = share(col(zo, core, 1), mate)
    products(zo, core, 0, 512)
    m_oa.wait_recv()
    m_ob.wait_recv()
    products(zo, mate_core, 0, 512)

    cp_tab.wait()
    cp_db.wait()
    dblk[NBL] = jnp.zeros((BS, BS), BF16)

    def out_copy(n, slot):
        return pltpu.make_async_copy(
            obuf.at[slot], grad_out.at[:, pl.ds(pl.multiple_of(n * TILE, TILE), TILE)], osem.at[slot])

    def tile(n):
        slot = n % 2
        if n + 1 < TILES:
            w_copy(n + 1, 1 - slot).start()
        w_copy(n, slot).wait()

        @pl.loop(0, CB)
        def _(c):
            for r in range(2):
                k = stab[0, (n * 2 + r) * CB + c]
                cols = pl.ds(pl.multiple_of(c * BS, BS), BS)
                wbuf[slot, r * BS:(r + 1) * BS, cols] += dblk[k]

        if n >= 2:
            out_copy(n - 2, slot).wait()

        @pl.loop(0, 2)
        def _(m):
            rows = pl.ds(pl.multiple_of(m * 256, 256), 256)
            obuf[slot, rows, :] = lax.dot_general(
                cbuf[rows, :], wbuf[slot], (((1,), (1,)), ((), ())), preferred_element_type=F32).astype(BF16)

        out_copy(n, slot).start()

    axes = ((xx, x_up, x_dn), (yy, y_up, y_dn))
    us = [(axes[h][0], axes[h][1], axes[h][2]) for h in range(2)]
    ws = [(axes[1 - h][0], axes[1 - h][1], axes[1 - h][2]) for h in range(2)]

    def fill(h, quarter, ab):
        @pl.loop(0, 8)
        def _(j):
            o, i = j // 2, lax.rem(j, 2)
            dev = o * 4 + quarter if h else quarter * 4 + o
            t = dev * CAP + h * 4 + ab * 2 + i
            stage[h, quarter, ab, o, i] = dense[stab[1, t]]

    s1 = [None, None]
    for h in range(2):
        u, up, dn = us[h]
        opp = mod4(u + 2)
        fill(h, opp, 0)
        a1 = send(stage.at[h, opp, 0], rx.at[h, 0], up)
        fill(h, opp, 1)
        b1 = send(stage.at[h, opp, 1], rx.at[h, 1], dn)
        s1[h] = [a1, b1]
    for h in range(2):
        u, up, dn = us[h]
        qu, qd = mod4(u + 1), mod4(u - 1)
        fill(h, qu, 1)
        a2 = send(stage.at[h, qu, 1], ry.at[h, 0, 1], up)
        fill(h, qd, 0)
        b2 = send(stage.at[h, qd, 0], ry.at[h, 1, 0], dn)
        s1[h] += [a2, b2]
    for h in range(2):
        u, up, dn = us[h]
        fill(h, mod4(u + 1), 0)
        fill(h, mod4(u - 1), 1)
        fill(h, u, 0)
        fill(h, u, 1)

    def add2(dst, a, b):
        @pl.loop(0, 4)
        def _(o):
            dst[o] = (a[o].astype(F32) + b[o].astype(F32)).astype(BF16)

    tile(0)
    tile(1)
    for h in range(2):
        u, up, dn = us[h]
        a1, b1, a2, b2 = s1[h]
        a1.wait_recv()
        add2(cb.at[h, 0], stage.at[h, mod4(u + 1), 0], rx.at[h, 0])
        a3 = send(cb.at[h, 0], ry.at[h, 0, 0], up)
        b1.wait_recv()
        add2(cb.at[h, 1], stage.at[h, mod4(u - 1), 1], rx.at[h, 1])
        b3 = send(cb.at[h, 1], ry.at[h, 1, 1], dn)
        s1[h] += [a3, b3]
    tile(2)
    tile(3)
    s2 = [None, None]
    for h in range(2):
        u, up, dn = us[h]
        w, wup, wdn = ws[h]
        a1, b1, a2, b2, a3, b3 = s1[h]
        for ab, pair in ((0, (a3, b2)), (1, (a2, b3))):
            for c in pair:
                c.wait_recv()

            @pl.loop(0, 4)
            def _(o):
                r1[h, ab, o] = (
                    stage[h, u, ab, o].astype(F32) + ry[h, 0, ab, o].astype(F32) + ry[h, 1, ab, o].astype(F32)
                ).astype(BF16)
        wopp, wqu, wqd = mod4(w + 2), mod4(w + 1), mod4(w - 1)
        s2[h] = [
            send(r1.at[h, 0, wopp], rx2.at[h, 0], wup),
            send(r1.at[h, 1, wopp], rx2.at[h, 1], wdn),
            send(r1.at[h, 1, wqu], ry2.at[h, 0, 1], wup),
            send(r1.at[h, 0, wqd], ry2.at[h, 1, 0], wdn),
        ]
    tile(4)
    for h in range(2):
        w, wup, wdn = ws[h]
        a1, b1, a2, b2 = s2[h]
        a1.wait_recv()
        cb2[h, 0] = (r1[h, 0, mod4(w + 1)].astype(F32) + rx2[h, 0].astype(F32)).astype(BF16)
        a3 = send(cb2.at[h, 0], ry2.at[h, 0, 0], wup)
        b1.wait_recv()
        cb2[h, 1] = (r1[h, 1, mod4(w - 1)].astype(F32) + rx2[h, 1].astype(F32)).astype(BF16)
        b3 = send(cb2.at[h, 1], ry2.at[h, 1, 1], wdn)
        s2[h] += [a3, b3]
    cp_dr.wait()
    hit16 = hit.astype(BF16)

    @pl.loop(0, 32)
    def _(i):
        lanes = pl.ds(pl.multiple_of(i * 512, 512), 512)
        cur[:, lanes] = jnp.dot(hit16, drow[:, lanes], preferred_element_type=F32)

    for h in range(2):
        w, wup, wdn = ws[h]
        a1, b1, a2, b2, a3, b3 = s2[h]
        for ab, pair in ((0, (a3, b2)), (1, (a2, b3))):
            for c in pair:
                c.wait_recv()
            for i in range(2):
                gsum[pl.ds((h * 4 + ab * 2 + i) * BS, BS), :] = (
                    r1[h, ab, w, i].astype(F32) + ry2[h, 0, ab, i].astype(F32) + ry2[h, 1, ab, i].astype(F32))
    cp_m.wait()
    cp_v.wait()

    def adam(r):
        lanes = pl.ds(pl.multiple_of(r * BS, BS), BS)
        g = gsum[pl.ds(r, CAP, stride=BS), :] * GRAD_SCALE
        m0, v0 = mbuf[:, lanes], vbuf[:, lanes]
        m1 = BETA_ONE * m0 + (1.0 - BETA_ONE) * g
        v1 = BETA_TWO * v0 + (1.0 - BETA_TWO) * g * g
        stepped = cur[0:CAP, lanes] - LEARN_RATE * (m1 / CORRECT_ONE) / (jnp.sqrt(v1 / CORRECT_TWO) + EPSILON)
        mnew[:, lanes] = jnp.where(filled, m1, m0)
        vnew[:, lanes] = jnp.where(filled, v1, v0)
        return jnp.where(filled, stepped, 0.0)

    g1 = [[], []]
    for h in range(2):
        group, member = (yy, xx) if h == 0 else (xx, yy)
        u, up, dn = us[h]
        for ab in range(2):
            @pl.loop(0, 16)
            def _(j):
                r = h * 32 + ab * 16 + j
                both = jnp.concatenate([adam(r), adam(r + 64)], axis=0).astype(BF16)
                gath[h, group, ab, member, :, pl.ds(pl.multiple_of(j * BS, BS), BS)] = both
            own = gath.at[h, group, ab, member]
            g1[h] += [send(own, own, up), send(own, own, dn)]
    out_m = local_copy(mnew, first_out, 7)
    out_v = local_copy(vnew, second_out, 8)
    tile(5)
    for h in range(2):
        group, member = (yy, xx) if h == 0 else (xx, yy)
        u, up, dn = us[h]
        up0, dn0, up1, dn1 = g1[h]
        up0.wait_recv()
        piece = gath.at[h, group, 0, mod4(member - 1)]
        f_up = send(piece, piece, up)
        dn1.wait_recv()
        piece = gath.at[h, group, 1, mod4(member + 1)]
        f_dn = send(piece, piece, dn)
        g1[h] += [f_up, f_dn]
    g2 = [[], []]
    for h in range(2):
        group = yy if h == 0 else xx
        w, wup, wdn = ws[h]
        up0, dn0, up1, dn1, f_up, f_dn = g1[h]
        dn0.wait_recv()
        f_up.wait_recv()
        piece = gath.at[h, group, 0]
        g2[h] += [send(piece, piece, wup), send(piece, piece, wdn)]
        up1.wait_recv()
        f_dn.wait_recv()
        piece = gath.at[h, group, 1]
        g2[h] += [send(piece, piece, wup), send(piece, piece, wdn)]
    tile(6)
    for h in range(2):
        group = yy if h == 0 else xx
        w, wup, wdn = ws[h]
        up0, dn0, up1, dn1 = g2[h]
        up0.wait_recv()
        piece = gath.at[h, mod4(group - 1), 0]
        f_up = send(piece, piece, wup)
        dn1.wait_recv()
        piece = gath.at[h, mod4(group + 1), 1]
        f_dn = send(piece, piece, wdn)
        g2[h] += [f_up, f_dn]

    for ab in range(2):
        for h in range(2):
            up0, dn0, up1, dn1, f_up, f_dn = g2[h]
            for c in ((dn0, f_up), (up1, f_dn))[ab]:
                c.wait_recv()

            @pl.loop(0, 4)
            def _(i):
                x = gath[h, :, ab, :, :, pl.ds(pl.multiple_of(i * 512, 512), 512)].reshape(256, 512)
                for half in range(2):
                    lanes = pl.ds(pl.multiple_of(half * 8192 + h * 4096 + ab * 2048 + i * 512, 512), 512)
                    dnew[:, lanes] = jnp.dot(pick[h, half], x, preferred_element_type=F32).astype(BF16)
    out_d = local_copy(dnew, deltas_out, 9)
    for c in sent:
        c.wait_send()
    out_m.wait()
    out_v.wait()
    out_copy(TILES - 2, (TILES - 2) % 2).wait()
    out_copy(TILES - 1, (TILES - 1) % 2).wait()
    out_d.wait()


def local(hidden_act, cotangent, weight, deltas, block_ids, owners, first_moment, second_moment):
    any_spec = pl.BlockSpec(memory_space=pl.ANY)
    vm_spec = pl.BlockSpec(memory_space=pltpu.VMEM)
    V = pltpu.VMEM
    outs = pl.pallas_call(
        kernel,
        out_shape=(
            jax.ShapeDtypeStruct((TOK, FFL), BF16),
            jax.ShapeDtypeStruct((NBL, BS * BS), BF16),
            jax.ShapeDtypeStruct((CAP, BS * BS), F32),
            jax.ShapeDtypeStruct((CAP, BS * BS), F32),
        ),
        in_specs=[any_spec] * 5 + [vm_spec] * 2 + [any_spec] * 2,
        out_specs=(any_spec,) * 4,
        scratch_shapes=[
            V((TOK, D), BF16),
            V((TOK, FFL), BF16),
            V((FFL, TOK), BF16),
            V((RB * CB, BS, BS), BF16),
            V((2, TILE, D), BF16),
            V((NBL, BS * BS), BF16),
            V((NBL + 1, BS, BS), BF16),
            V((2, 4, 2, 4, 2, BS, BS), BF16),
            V((2, 2, 4, 2, BS, BS), BF16),
            V((2, 2, 2, 4, 2, BS, BS), BF16),
            V((2, 2, 4, 2, BS, BS), BF16),
            V((2, 2, 4, 2, BS, BS), BF16),
            V((2, 2, 2, BS, BS), BF16),
            V((2, 2, 2, 2, BS, BS), BF16),
            V((2, 2, 2, BS, BS), BF16),
            V((CAP * BS, BS), F32),
            V((2, 4, 2, 4, 16, 2048), BF16),
            V((CAP, BS * BS), F32),
            V((CAP, BS * BS), F32),
            V((CAP, BS * BS), F32),
            V((CAP, BS * BS), F32),
            V((16, BS * BS), F32),
            V((NBL, BS * BS), BF16),
            V((2, TOK, TILE), BF16),
            V((8, 512), I32),
            pltpu.SMEM((8, 512), I32),
            V((2, 2, NBL, 256), BF16),
            pltpu.SemaphoreType.DMA((10,)),
            pltpu.SemaphoreType.DMA((2,)),
            pltpu.SemaphoreType.DMA((2,)),
            pltpu.SemaphoreType.DMA((N_REMOTE,)),
            pltpu.SemaphoreType.DMA((N_REMOTE,)),
        ],
        compiler_params=pltpu.CompilerParams(
            collective_id=0, has_side_effects=True, vmem_limit_bytes=60 * 1024 * 1024),
        cost_estimate=pl.CostEstimate(flops=15 * 10**9, bytes_accessed=25 * 10**6, transcendentals=0),
    )(
        cotangent, hidden_act, weight, deltas, deltas.reshape(NBL, BS, BS),
        block_ids.reshape(1, NBL), owners.reshape(1, NBL), first_moment[0], second_moment[0],
    )
    input_grad, new_deltas, new_first, new_second = outs
    return (input_grad, new_deltas, new_first[None], new_second[None])


def solution(mesh):
    in_specs = (
        P("dp", "mp"),
        P("dp", "mp"),
        P("mp", None),
        P("mp", None),
        P("mp"),
        P("mp", None),
        P("mp", "dp", None),
        P("mp", "dp", None),
    )
    out_specs = (P("dp", "mp"), P("mp", None), P("mp", "dp", None), P("mp", "dp", None))
    return jax.shard_map(local, mesh=mesh, in_specs=in_specs, out_specs=out_specs, check_vma=False)
```

```python
import functools
import math

import jax
import jax.numpy as jnp
from jax import lax
from jax.experimental import pallas as pl
from jax.experimental.pallas import tpu as pltpu
from jax.sharding import PartitionSpec as P

D = 4096
BS = 128
TOK = 512
FFL = 1792
RB = 14
CB = 32
NBL = 64
CAP = 8
TILES = 7
TILE = FFL // TILES

BETA_ONE = 0.9
BETA_TWO = 0.95
LEARN_RATE = 0.02
EPSILON = 1e-08
CORRECT_ONE = 1.0 - 0.9**4
CORRECT_TWO = 1.0 - 0.95**4
GRAD_SCALE = 1.0 / math.sqrt(8192.0)

MESH = pl.DeviceIdType.MESH
BF16, F32, I32 = jnp.bfloat16, jnp.float32, jnp.int32
N_REMOTE = 80


def mod4(v):
    return lax.rem(v + 4, 4)


def kernel(
    cot, hid, weight, deltas, ids_row, own_row, first, second,
    grad_out, deltas_out, first_out, second_out,
    cbuf, hbuf, ht, dense, wbuf, drow, dblk, stage, rx, ry, cb, r1, ry2, gsum,
    agm, sbm, rbm, agg, sbg, rbg, gath, g16, cur, mbuf, vbuf, mnew, vnew, dnew, obuf, tab, stab,
    sel_m, sel_g, sel_d, lsem, wsem, osem, dsem, ssem, rsem,
):
    dp, mp = lax.axis_index("dp"), lax.axis_index("mp")
    xx, yy = dp // 4, lax.rem(dp, 4)
    zz, core = mp // 2, lax.rem(mp, 2)
    x_dev = [(mod4(xx + d) * 4 + yy, mp) for d in range(4)]
    y_dev = [(xx * 4 + mod4(yy + d), mp) for d in range(4)]
    z_up, z_dn = (dp, mod4(zz + 1) * 2 + core), (dp, mod4(zz - 1) * 2 + core)
    mate = (dp, zz * 2 + 1 - core)
    us = ((xx, x_dev), (yy, y_dev))
    ws = ((yy, y_dev), (xx, x_dev))

    def local_copy(src, dst, i):
        c = pltpu.make_async_copy(src, dst, lsem.at[i])
        c.start()
        return c

    def col(z, c, half, width=256):
        return pl.ds(pl.multiple_of((z * 2 + c) * 512 + half * 256, 256), width)

    cp_cot = local_copy(cot, cbuf.at[:, col(zz, core, 0, 512)], 0)
    cp_m = local_copy(first, mbuf, 3)
    cp_v = local_copy(second, vbuf, 4)
    cp_hid = local_copy(hid, hbuf, 1)
    cp_dr = local_copy(deltas, drow, 2)

    def w_copy(n, slot):
        return pltpu.make_async_copy(
            weight.at[pl.ds(pl.multiple_of(n * TILE, TILE), TILE)], wbuf.at[slot], wsem.at[slot])

    w_copy(0, 0).start()

    barrier = pltpu.get_barrier_semaphore()
    for dev in (*x_dev[1:], *y_dev[1:], z_up, z_dn, mate):
        pl.semaphore_signal(barrier, inc=1, device_id=dev, device_id_type=MESH)
    pl.semaphore_wait(barrier, 9)

    sent = []

    def send(src, dst, dev):
        i = len(sent)
        c = pltpu.make_async_remote_copy(
            src_ref=src, dst_ref=dst, send_sem=ssem.at[i], recv_sem=rsem.at[i],
            device_id=dev, device_id_type=MESH)
        c.start()
        sent.append(c)
        return c

    def share(where, dev):
        return send(cbuf.at[:, where], cbuf.at[:, where], dev)

    cp_cot.wait()
    up_a = share(col(zz, core, 0), z_up)
    dn_b = share(col(zz, core, 1), z_dn)
    to_mate = share(col(zz, core, 0, 512), mate)
    up_b = share(col(zz, core, 1), z_up)
    dn_a = share(col(zz, core, 0), z_dn)

    cp_m.wait()
    cp_v.wait()
    m1 = [None, None]
    for h in range(2):
        u, dev = us[h]
        for ab in range(2):
            @pl.loop(0, 8)
            def _(j):
                here = pl.ds(pl.multiple_of(j * 512, 512), 512)
                there = pl.ds(pl.multiple_of(h * 8192 + ab * 4096 + j * 512, 512), 512)
                agm[h, ab, u, :, here] = jnp.concatenate([mbuf[:, there], vbuf[:, there]], axis=0).astype(BF16)
        own = [agm.at[h, ab, u] for ab in range(2)]
        m1[h] = [send(own[0], own[0], dev[1]), send(own[1], own[1], dev[3]),
                 send(own[1], own[1], dev[1]), send(own[0], own[0], dev[3])]

    ri = lax.broadcasted_iota(I32, (NBL, NBL), 0)
    ci = lax.broadcasted_iota(I32, (NBL, NBL), 1)
    eye = ri == ci
    owns = jnp.broadcast_to(own_row[...], (NBL, NBL))
    own_col = jnp.sum(jnp.where(eye, owns, 0), axis=1, keepdims=True)
    ids_col = jnp.sum(jnp.where(eye, jnp.broadcast_to(ids_row[...], (NBL, NBL)), 0), axis=1, keepdims=True)
    slot_col = jnp.sum(jnp.where((own_col == owns) & (ci < ri), 1, 0), axis=1, keepdims=True)
    target_col = own_col * CAP + slot_col
    target_row = jnp.sum(jnp.where(eye, jnp.broadcast_to(target_col, (NBL, NBL)), 0), axis=0, keepdims=True)
    block_at = lax.broadcasted_iota(I32, (NBL, 512), 1)
    number = lax.broadcasted_iota(I32, (NBL, 512), 0)
    inverse = NBL - jnp.max(jnp.where(ids_col == block_at, NBL - number, 0), axis=0, keepdims=True)
    tab[...] = jnp.zeros_like(tab)
    tab[0:1, :] = inverse
    tab[1:2, 0:NBL] = ids_row[...]
    cp_tab = local_copy(tab, stab, 5)

    def one_hot(mask):
        return jnp.where(mask, 1.0, 0.0).astype(BF16)

    mine = lax.broadcasted_iota(I32, (16, NBL), 0)
    filled = jnp.max(jnp.where(target_row == dp * CAP + mine, 1, 0), axis=1, keepdims=True)[0:CAP] > 0
    for h in range(2):
        def dev_mem(v):
            return xx * 4 + v if h else v * 4 + yy

        def dev_dest(v):
            return v * 4 + yy if h else xx * 4 + v

        k = dev_dest(ri >> 4) * 4 + (ri & 3)
        wanted = jnp.sum(jnp.where(ci == k, jnp.broadcast_to(target_row, (NBL, NBL)), 0), axis=1, keepdims=True)
        hit = (wanted == dev_mem(ci >> 4) * CAP + (ci & 7)) & (((ri >> 3) & 1) == ((ci >> 3) & 1))
        for half in range(2):
            sel_m[h, half] = one_hot(hit & (((ri >> 2) & 1) == half))
        k = dev_mem(ci >> 4) * 4 + (ci & 3)
        goes = jnp.sum(jnp.where(ri == k, jnp.broadcast_to(target_col, (NBL, NBL)), 0), axis=0, keepdims=True)
        rg = lax.broadcasted_iota(I32, (128, NBL), 0)
        cg = lax.broadcasted_iota(I32, (128, NBL), 1)
        sel_g[h] = one_hot((goes == dev_dest(rg >> 5) * CAP + (rg & 7)) & (((rg >> 3) & 3) == ((cg >> 2) & 3)))
        rd = lax.broadcasted_iota(I32, (256, 256), 0)
        cd = lax.broadcasted_iota(I32, (256, 256), 1)
        group, mem = cd >> 6, (cd >> 4) & 3
        dev = group * 4 + mem if h else mem * 4 + group
        sel_d[h] = one_hot(((rd & 63) == dev * 4 + (cd & 3)) & ((rd >> 6) == ((cd >> 2) & 3)))

    cp_hid.wait()

    @pl.loop(0, TILES)
    def _(i):
        rows = pl.ds(pl.multiple_of(i * TILE, TILE), TILE)
        ht[rows, :] = hbuf[:, rows].T

    def products(z, c, half, width):
        first_col = (z * 2 + c) * 4 + half * 2
        where = col(z, c, half, width)

        @pl.loop(0, TILES)
        def _(i):
            rows = pl.ds(pl.multiple_of(i * TILE, TILE), TILE)
            g = jnp.dot(ht[rows, :], cbuf[:, where], preferred_element_type=F32).astype(BF16)
            for r in range(2):
                for k in range(width // BS):
                    dense[(i * 2 + r) * CB + first_col + k] = g[r * BS:(r + 1) * BS, k * BS:(k + 1) * BS]

    mate_core = 1 - core
    zu, zd, zo = mod4(zz + 1), mod4(zz - 1), mod4(zz + 2)
    products(zz, core, 0, 512)
    for h in range(2):
        u, dev = us[h]
        m1[h][0].wait_recv()
        piece = agm.at[h, 0, mod4(u - 1)]
        f_up = send(piece, piece, dev[1])
        m1[h][1].wait_recv()
        piece = agm.at[h, 1, mod4(u + 1)]
        f_dn = send(piece, piece, dev[3])
        m1[h] += [f_up, f_dn]
    to_mate.wait_recv()
    products(zz, mate_core, 0, 512)
    up_a.wait_recv()
    fw_a = share(col(zd, core, 0), z_up)
    m_da = share(col(zd, core, 0), mate)
    dn_b.wait_recv()
    fw_b = share(col(zu, core, 1), z_dn)
    m_ub = share(col(zu, core, 1), mate)
    products(zd, core, 0, 256)
    products(zu, core, 1, 256)
    m_da.wait_recv()
    products(zd, mate_core, 0, 256)
    m_ub.wait_recv()
    products(zu, mate_core, 1, 256)

    m2 = [None, None]
    for h in range(2):
        for c in m1[h][2:]:
            c.wait_recv()

        @pl.loop(0, 8)
        def _(j):
            here = pl.ds(pl.multiple_of(j * 512, 512), 512)
            both = 0.0
            for ab in range(2):
                x = agm[h, ab, :, :, here].reshape(64, 512)
                both = both + jnp.dot(sel_m[h, ab], x, preferred_element_type=F32)
            sbm[h, :, :, here] = both.astype(BF16).reshape(4, 16, 512)
        w, dev = ws[h]
        m2[h] = [send(sbm.at[h, mod4(w + d)], rbm.at[h, d], dev[d]) for d in (1, 3, 2)]

    up_b.wait_recv()
    m_db = share(col(zd, core, 1), mate)
    dn_a.wait_recv()
    m_ua = share(col(zu, core, 0), mate)
    products(zd, core, 1, 256)
    products(zu, core, 0, 256)
    m_db.wait_recv()
    products(zd, mate_core, 1, 256)
    m_ua.wait_recv()
    products(zu, mate_core, 0, 256)

    cp_dr.wait()
    rc = lax.broadcasted_iota(I32, (16, NBL), 0)
    cc = lax.broadcasted_iota(I32, (16, NBL), 1)
    my_row = cc == dp * 4 + (rc & 3)

    @pl.loop(0, 8)
    def _(j):
        here = pl.ds(pl.multiple_of(j * 512, 512), 512)
        rows = 0.0
        for quarter in range(4):
            there = pl.ds(pl.multiple_of(quarter * 4096 + j * 512, 512), 512)
            pick = one_hot(my_row & ((rc >> 2) == quarter))
            rows = rows + jnp.dot(pick, drow[:, there], preferred_element_type=F32)
        cur[:, here] = rows

    by_row = dblk.reshape((NBL + 1) * BS, BS)

    @pl.loop(0, BS)
    def _(r):
        by_row[pl.ds(r, NBL, stride=BS), :] = drow[:, pl.ds(pl.multiple_of(r * BS, BS), BS)].astype(F32)

    dblk[NBL] = jnp.zeros((BS, BS), F32)

    fw_a.wait_recv()
    m_oa = share(col(zo, core, 0), mate)
    fw_b.wait_recv()
    m_ob = share(col(zo, core, 1), mate)
    products(zo, core, 0, 512)
    m_oa.wait_recv()
    m_ob.wait_recv()
    products(zo, mate_core, 0, 512)
    cp_tab.wait()

    def out_copy(n, slot):
        return pltpu.make_async_copy(
            obuf.at[slot], grad_out.at[:, pl.ds(pl.multiple_of(n * TILE, TILE), TILE)], osem.at[slot])

    def tile(n):
        slot = n % 2
        if n + 1 < TILES:
            w_copy(n + 1, 1 - slot).start()
        w_copy(n, slot).wait()

        @pl.loop(0, CB)
        def _(c):
            for r in range(2):
                k = stab[0, (n * 2 + r) * CB + c]
                cols = pl.ds(pl.multiple_of(c * BS, BS), BS)
                add = dblk[k]
                old = wbuf[slot, r * BS:(r + 1) * BS, cols]
                wbuf[slot, r * BS:(r + 1) * BS, cols] = (old.astype(F32) + add).astype(BF16)

        if n >= 2:
            out_copy(n - 2, slot).wait()

        @pl.loop(0, 2)
        def _(m):
            rows = pl.ds(pl.multiple_of(m * 256, 256), 256)
            obuf[slot, rows, :] = lax.dot_general(
                cbuf[rows, :], wbuf[slot], (((1,), (1,)), ((), ())), preferred_element_type=F32).astype(BF16)

        out_copy(n, slot).start()

    def fill(h, quarter, ab):
        @pl.loop(0, 4)
        def _(o):
            dev = o * 4 + quarter if h else quarter * 4 + o
            stage[h, quarter, ab, o] = dense[stab[1, dev * 4 + h * 2 + ab]]

    s1 = [None, None]
    for h in range(2):
        u, dev = us[h]
        opp = mod4(u + 2)
        fill(h, opp, 0)
        a1 = send(stage.at[h, opp, 0], rx.at[h, 0], dev[1])
        fill(h, opp, 1)
        b1 = send(stage.at[h, opp, 1], rx.at[h, 1], dev[3])
        s1[h] = [a1, b1]
    for h in range(2):
        u, dev = us[h]
        qu, qd = mod4(u + 1), mod4(u - 1)
        fill(h, qu, 1)
        a2 = send(stage.at[h, qu, 1], ry.at[h, 0, 1], dev[1])
        fill(h, qd, 0)
        b2 = send(stage.at[h, qd, 0], ry.at[h, 1, 0], dev[3])
        s1[h] += [a2, b2]
    for h in range(2):
        u, dev = us[h]
        fill(h, mod4(u + 1), 0)
        fill(h, mod4(u - 1), 1)
        fill(h, u, 0)
        fill(h, u, 1)

    def add2(dst, a, b):
        @pl.loop(0, 4)
        def _(o):
            dst[o] = (a[o].astype(F32) + b[o].astype(F32)).astype(BF16)

    tile(0)
    tile(1)
    for h in range(2):
        u, dev = us[h]
        a1, b1, a2, b2 = s1[h]
        a1.wait_recv()
        add2(cb.at[h, 0], stage.at[h, mod4(u + 1), 0], rx.at[h, 0])
        a3 = send(cb.at[h, 0], ry.at[h, 0, 0], dev[1])
        b1.wait_recv()
        add2(cb.at[h, 1], stage.at[h, mod4(u - 1), 1], rx.at[h, 1])
        b3 = send(cb.at[h, 1], ry.at[h, 1, 1], dev[3])
        s1[h] += [a3, b3]
    tile(2)
    s2 = [None, None]
    for h in range(2):
        u, dev = us[h]
        w, wdev = ws[h]
        a1, b1, a2, b2, a3, b3 = s1[h]
        for ab, pair in ((0, (a3, b2)), (1, (a2, b3))):
            for c in pair:
                c.wait_recv()

            @pl.loop(0, 4)
            def _(o):
                r1[h, o, ab] = (
                    stage[h, u, ab, o].astype(F32) + ry[h, 0, ab, o].astype(F32) + ry[h, 1, ab, o].astype(F32)
                ).astype(BF16)
        s2[h] = [send(r1.at[h, mod4(w + d)], ry2.at[h, d], wdev[d]) for d in (1, 3, 2)]
    tile(3)
    for h in range(2):
        w, wdev = ws[h]
        for c in s2[h]:
            c.wait_recv()
        for ab in range(2):
            total = r1[h, w, ab].astype(F32)
            for d in (1, 2, 3):
                total = total + ry2[h, d, ab].astype(F32)
            gsum[pl.ds((h * 2 + ab) * BS, BS), :] = total * GRAD_SCALE

    g1 = [None, None]
    for h in range(2):
        u, dev = us[h]

        @pl.loop(0, 16)
        def _(j):
            rows = jnp.concatenate([gsum[pl.ds(quarter * 32 + h * 16 + j, 4, stride=BS), :] for quarter in range(4)], axis=0)
            g16[:, pl.ds(pl.multiple_of(h * 2048 + j * BS, BS), BS)] = rows
            agg[h, u, :, pl.ds(pl.multiple_of(j * BS, BS), BS)] = rows.astype(BF16)
        own = agg.at[h, u]
        g1[h] = [send(own, own, dev[d]) for d in (1, 3, 2)]

    def adam(g, m0, v0):
        m = BETA_ONE * m0 + (1.0 - BETA_ONE) * g
        v = BETA_TWO * v0 + (1.0 - BETA_TWO) * g * g
        return m, v

    for h in range(2):
        for c in m2[h]:
            c.wait_recv()
    d1 = [None, None]
    for h in range(2):
        u, dev = us[h]
        w, wdev = ws[h]

        @pl.loop(0, 16)
        def _(j):
            here = pl.ds(pl.multiple_of(h * 2048 + j * BS, BS), BS)
            parts = []
            for hm in range(2):
                got = sbm[hm, ws[hm][0], :, here].astype(F32)
                for d in (1, 2, 3):
                    got = got + rbm[hm, d, :, here].astype(F32)
                parts.append(got)
            m0 = jnp.concatenate([p[0:8] for p in parts], axis=0)
            v0 = jnp.concatenate([p[8:16] for p in parts], axis=0)
            m, v = adam(g16[:, here], m0, v0)
            new = cur[:, here] - LEARN_RATE * (m / CORRECT_ONE) / (jnp.sqrt(v / CORRECT_TWO) + EPSILON)
            gath[h, w, u, :, pl.ds(pl.multiple_of(j * BS, BS), BS)] = new.astype(BF16)
        own = gath.at[h, w, u]
        d1[h] = [send(own, own, dev[d]) for d in (1, 3, 2)]

    g2, d2 = [None, None], [None, None]
    for h in range(2):
        for c in g1[h]:
            c.wait_recv()

        @pl.loop(0, 4)
        def _(j):
            here = pl.ds(pl.multiple_of(j * 512, 512), 512)
            x = agg[h, :, :, here].reshape(64, 512)
            sbg[h, :, :, here] = jnp.dot(sel_g[h], x, preferred_element_type=F32).astype(BF16).reshape(4, 32, 512)
    for h in range(2):
        w, dev = ws[h]
        for c in d1[h]:
            c.wait_recv()
        lo, hi = gath.at[h, w, pl.ds(0, 2)], gath.at[h, w, pl.ds(2, 2)]
        d2[h] = [send(lo, lo, dev[1]), send(hi, hi, dev[3])]
    for h in range(2):
        w, dev = ws[h]
        g2[h] = [send(sbg.at[h, mod4(w + d)], rbg.at[h, d], dev[d]) for d in (1, 3, 2)]
        lo, hi = gath.at[h, w, pl.ds(0, 2)], gath.at[h, w, pl.ds(2, 2)]
        d2[h] += [send(hi, hi, dev[1]), send(lo, lo, dev[3])]
    tile(4)
    for h in range(2):
        w, dev = ws[h]
        d2[h][0].wait_recv()
        piece = gath.at[h, mod4(w - 1), pl.ds(0, 2)]
        f_up = send(piece, piece, dev[1])
        d2[h][1].wait_recv()
        piece = gath.at[h, mod4(w + 1), pl.ds(2, 2)]
        f_dn = send(piece, piece, dev[3])
        d2[h] += [f_up, f_dn]
    tile(5)
    for h in range(2):
        w, dev = ws[h]
        for c in g2[h]:
            c.wait_recv()

        @pl.loop(0, 16)
        def _(j):
            here = pl.ds(pl.multiple_of(j * BS, BS), BS)
            got = sbg[h, w, :, here].astype(F32)
            for d in (1, 2, 3):
                got = got + rbg[h, d, :, here].astype(F32)
            for quarter in range(4):
                lanes = pl.ds(pl.multiple_of(quarter * 4096 + h * 2048 + j * BS, BS), BS)
                m0, v0 = mbuf[:, lanes], vbuf[:, lanes]
                m, v = adam(got[quarter * 8:quarter * 8 + 8], m0, v0)
                mnew[:, lanes] = jnp.where(filled, m, m0)
                vnew[:, lanes] = jnp.where(filled, v, v0)
    out_m = local_copy(mnew, first_out, 6)
    out_v = local_copy(vnew, second_out, 7)
    tile(6)
    outs = []
    for h in range(2):
        for c in d2[h][2:]:
            c.wait_recv()

        @pl.loop(0, 4)
        def _(j):
            x = gath[h, :, :, :, pl.ds(pl.multiple_of(j * 512, 512), 512)].reshape(256, 512)
            y = jnp.dot(sel_d[h], x, preferred_element_type=F32).astype(BF16)
            for quarter in range(4):
                lanes = pl.ds(pl.multiple_of(quarter * 4096 + h * 2048 + j * 512, 512), 512)
                dnew[:, lanes] = y[quarter * 64:(quarter + 1) * 64]
        for quarter in range(4):
            lanes = pl.ds(quarter * 4096 + h * 2048, 2048)
            c = pltpu.make_async_copy(dnew.at[:, lanes], deltas_out.at[:, lanes], dsem.at[h * 4 + quarter])
            c.start()
            outs.append(c)
    for c in sent:
        c.wait_send()
    out_m.wait()
    out_v.wait()
    out_copy(TILES - 2, (TILES - 2) % 2).wait()
    out_copy(TILES - 1, (TILES - 1) % 2).wait()
    for c in outs:
        c.wait()


def local(hidden_act, cotangent, weight, deltas, block_ids, owners, first_moment, second_moment):
    any_spec = pl.BlockSpec(memory_space=pl.ANY)
    vm_spec = pl.BlockSpec(memory_space=pltpu.VMEM)
    V = pltpu.VMEM
    outs = pl.pallas_call(
        kernel,
        out_shape=(
            jax.ShapeDtypeStruct((TOK, FFL), BF16),
            jax.ShapeDtypeStruct((NBL, BS * BS), BF16),
            jax.ShapeDtypeStruct((CAP, BS * BS), F32),
            jax.ShapeDtypeStruct((CAP, BS * BS), F32),
        ),
        in_specs=[any_spec] * 4 + [vm_spec] * 2 + [any_spec] * 2,
        out_specs=(any_spec,) * 4,
        scratch_shapes=[
            V((TOK, D), BF16),
            V((TOK, FFL), BF16),
            V((FFL, TOK), BF16),
            V((RB * CB, BS, BS), BF16),
            V((2, TILE, D), BF16),
            V((NBL, BS * BS), BF16),
            V((NBL + 1, BS, BS), F32),
            V((2, 4, 2, 4, BS, BS), BF16),
            V((2, 2, 4, BS, BS), BF16),
            V((2, 2, 2, 4, BS, BS), BF16),
            V((2, 2, 4, BS, BS), BF16),
            V((2, 4, 2, BS, BS), BF16),
            V((2, 4, 2, BS, BS), BF16),
            V((4 * BS, BS), F32),
            V((2, 2, 4, 16, 4096), BF16),
            V((2, 4, 16, 4096), BF16),
            V((2, 4, 16, 4096), BF16),
            V((2, 4, 16, 2048), BF16),
            V((2, 4, 32, 2048), BF16),
            V((2, 4, 32, 2048), BF16),
            V((2, 4, 4, 16, 2048), BF16),
            V((16, 4096), F32),
            V((16, 4096), F32),
            V((CAP, BS * BS), F32),
            V((CAP, BS * BS), F32),
            V((CAP, BS * BS), F32),
            V((CAP, BS * BS), F32),
            V((NBL, BS * BS), BF16),
            V((2, TOK, TILE), BF16),
            V((8, 512), I32),
            pltpu.SMEM((8, 512), I32),
            V((2, 2, 64, 64), BF16),
            V((2, 128, 64), BF16),
            V((2, 256, 256), BF16),
            pltpu.SemaphoreType.DMA((8,)),
            pltpu.SemaphoreType.DMA((2,)),
            pltpu.SemaphoreType.DMA((2,)),
            pltpu.SemaphoreType.DMA((8,)),
            pltpu.SemaphoreType.DMA((N_REMOTE,)),
            pltpu.SemaphoreType.DMA((N_REMOTE,)),
        ],
        compiler_params=pltpu.CompilerParams(
            collective_id=0, has_side_effects=True, vmem_limit_bytes=60 * 1024 * 1024),
        cost_estimate=pl.CostEstimate(flops=15 * 10**9, bytes_accessed=25 * 10**6, transcendentals=0),
    )(
        cotangent, hidden_act, weight, deltas,
        block_ids.reshape(1, NBL), owners.reshape(1, NBL), first_moment[0], second_moment[0],
    )
    input_grad, new_deltas, new_first, new_second = outs
    return (input_grad, new_deltas, new_first[None], new_second[None])


def solution(mesh):
    in_specs = (
        P("dp", "mp"),
        P("dp", "mp"),
        P("mp", None),
        P("mp", None),
        P("mp"),
        P("mp", None),
        P("mp", "dp", None),
        P("mp", "dp", None),
    )
    out_specs = (P("dp", "mp"), P("mp", None), P("mp", "dp", None), P("mp", "dp", None))
    return jax.shard_map(local, mesh=mesh, in_specs=in_specs, out_specs=out_specs, check_vma=False)
```

```python
import functools
import math

import jax
import jax.numpy as jnp
from jax import lax
from jax.experimental import pallas as pl
from jax.experimental.pallas import tpu as pltpu
from jax.sharding import PartitionSpec as P

D = 4096
BS = 128
TOK = 512
FFL = 1792
RB = 14
CB = 32
NBL = 64
CAP = 8
TILES = 7
TILE = FFL // TILES

BETA_ONE = 0.9
BETA_TWO = 0.95
LEARN_RATE = 0.02
EPSILON = 1e-08
CORRECT_ONE = 1.0 - 0.9**4
CORRECT_TWO = 1.0 - 0.95**4
GRAD_SCALE = 1.0 / math.sqrt(8192.0)

MESH = pl.DeviceIdType.MESH
BF16, F32, I32 = jnp.bfloat16, jnp.float32, jnp.int32
N_REMOTE = 96


def mod4(v):
    return lax.rem(v + 4, 4)


def kernel(
    cot, hid, weight, deltas, ids_row, own_row, first, second,
    grad_out, deltas_out, first_out, second_out,
    cbuf, hbuf, ht, dense, wbuf, drow, dwide, dblk, stage, rx, ry, cb, r1, ry2, gsum,
    agm, sbm, rbm, agg, sbg, rbg, gath, g16, cur, mbuf, vbuf, mnew, vnew, dnew, obuf, tab, stab,
    sel_m, sel_g, sel_d, lsem, wsem, osem, dsem, ssem, rsem,
):
    dp, mp = lax.axis_index("dp"), lax.axis_index("mp")
    xx, yy = dp // 4, lax.rem(dp, 4)
    zz, core = mp // 2, lax.rem(mp, 2)
    x_dev = [(mod4(xx + d) * 4 + yy, mp) for d in range(4)]
    y_dev = [(xx * 4 + mod4(yy + d), mp) for d in range(4)]
    z_up, z_dn = (dp, mod4(zz + 1) * 2 + core), (dp, mod4(zz - 1) * 2 + core)
    mate = (dp, zz * 2 + 1 - core)
    us = ((xx, x_dev), (yy, y_dev))
    ws = ((yy, y_dev), (xx, x_dev))

    def local_copy(src, dst, i):
        c = pltpu.make_async_copy(src, dst, lsem.at[i])
        c.start()
        return c

    def col(z, c, half, width=256):
        return pl.ds(pl.multiple_of((z * 2 + c) * 512 + half * 256, 256), width)

    cp_cot = local_copy(cot, cbuf.at[:, col(zz, core, 0, 512)], 0)
    cp_m = local_copy(first, mbuf, 3)
    cp_v = local_copy(second, vbuf, 4)
    cp_hid = local_copy(hid, hbuf, 1)
    cp_dr = local_copy(deltas, drow, 2)

    def w_copy(n, slot):
        return pltpu.make_async_copy(
            weight.at[pl.ds(pl.multiple_of(n * TILE, TILE), TILE)], wbuf.at[slot], wsem.at[slot])

    w_copy(0, 0).start()

    barrier = pltpu.get_barrier_semaphore()
    for dev in (*x_dev[1:], *y_dev[1:], z_up, z_dn, mate):
        pl.semaphore_signal(barrier, inc=1, device_id=dev, device_id_type=MESH)
    pl.semaphore_wait(barrier, 9)

    sent = []

    def send(src, dst, dev):
        i = len(sent)
        c = pltpu.make_async_remote_copy(
            src_ref=src, dst_ref=dst, send_sem=ssem.at[i], recv_sem=rsem.at[i],
            device_id=dev, device_id_type=MESH)
        c.start()
        sent.append(c)
        return c

    def share(where, dev):
        return send(cbuf.at[:, where], cbuf.at[:, where], dev)

    cp_cot.wait()
    up_a = share(col(zz, core, 0), z_up)
    dn_b = share(col(zz, core, 1), z_dn)
    to_mate = share(col(zz, core, 0, 512), mate)
    up_b = share(col(zz, core, 1), z_up)
    dn_a = share(col(zz, core, 0), z_dn)

    cp_m.wait()
    cp_v.wait()
    m1 = [None, None]
    for h in range(2):
        u, dev = us[h]
        for ab in range(2):
            @pl.loop(0, 8)
            def _(j):
                here = pl.ds(pl.multiple_of(j * 512, 512), 512)
                there = pl.ds(pl.multiple_of(h * 8192 + ab * 4096 + j * 512, 512), 512)
                agm[h, ab, u, :, here] = jnp.concatenate([mbuf[:, there], vbuf[:, there]], axis=0).astype(BF16)
        own = [agm.at[h, ab, u] for ab in range(2)]
        m1[h] = [send(own[0], own[0], dev[1]), send(own[1], own[1], dev[3]),
                 send(own[1], own[1], dev[1]), send(own[0], own[0], dev[3])]

    ri = lax.broadcasted_iota(I32, (NBL, NBL), 0)
    ci = lax.broadcasted_iota(I32, (NBL, NBL), 1)
    eye = ri == ci
    owns = jnp.broadcast_to(own_row[...], (NBL, NBL))
    own_col = jnp.sum(jnp.where(eye, owns, 0), axis=1, keepdims=True)
    ids_col = jnp.sum(jnp.where(eye, jnp.broadcast_to(ids_row[...], (NBL, NBL)), 0), axis=1, keepdims=True)
    slot_col = jnp.sum(jnp.where((own_col == owns) & (ci < ri), 1, 0), axis=1, keepdims=True)
    target_col = own_col * CAP + slot_col
    target_row = jnp.sum(jnp.where(eye, jnp.broadcast_to(target_col, (NBL, NBL)), 0), axis=0, keepdims=True)
    block_at = lax.broadcasted_iota(I32, (NBL, 512), 1)
    number = lax.broadcasted_iota(I32, (NBL, 512), 0)
    inverse = NBL - jnp.max(jnp.where(ids_col == block_at, NBL - number, 0), axis=0, keepdims=True)
    tab[...] = jnp.zeros_like(tab)
    tab[0:1, :] = inverse
    tab[1:2, 0:NBL] = ids_row[...]
    cp_tab = local_copy(tab, stab, 5)

    def one_hot(mask):
        return jnp.where(mask, 1.0, 0.0).astype(BF16)

    mine = lax.broadcasted_iota(I32, (16, NBL), 0)
    filled = jnp.max(jnp.where(target_row == dp * CAP + mine, 1, 0), axis=1, keepdims=True)[0:CAP] > 0
    for h in range(2):
        def dev_mem(v):
            return xx * 4 + v if h else v * 4 + yy

        def dev_dest(v):
            return v * 4 + yy if h else xx * 4 + v

        k = dev_dest(ri >> 4) * 4 + (ri & 3)
        wanted = jnp.sum(jnp.where(ci == k, jnp.broadcast_to(target_row, (NBL, NBL)), 0), axis=1, keepdims=True)
        hit = (wanted == dev_mem(ci >> 4) * CAP + (ci & 7)) & (((ri >> 3) & 1) == ((ci >> 3) & 1))
        for half in range(2):
            sel_m[h, half] = one_hot(hit & (((ri >> 2) & 1) == half))
        k = dev_mem(ci >> 4) * 4 + (ci & 3)
        goes = jnp.sum(jnp.where(ri == k, jnp.broadcast_to(target_col, (NBL, NBL)), 0), axis=0, keepdims=True)
        rg = lax.broadcasted_iota(I32, (128, NBL), 0)
        cg = lax.broadcasted_iota(I32, (128, NBL), 1)
        sel_g[h] = one_hot((goes == dev_dest(rg >> 5) * CAP + (rg & 7)) & (((rg >> 3) & 3) == ((cg >> 2) & 3)))
        rd = lax.broadcasted_iota(I32, (256, 256), 0)
        cd = lax.broadcasted_iota(I32, (256, 256), 1)
        group, mem = cd >> 6, (cd >> 4) & 3
        dev = group * 4 + mem if h else mem * 4 + group
        sel_d[h] = one_hot(((rd & 63) == dev * 4 + (cd & 3)) & ((rd >> 6) == ((cd >> 2) & 3)))

    cp_hid.wait()

    @pl.loop(0, TILES)
    def _(i):
        rows = pl.ds(pl.multiple_of(i * TILE, TILE), TILE)
        ht[rows, :] = hbuf[:, rows].T

    def products(z, c, half):
        first_col = (z * 2 + c) * 4 + half * 2
        g = jnp.dot(ht[...], cbuf[:, col(z, c, half)], preferred_element_type=F32).astype(BF16)
        for r in range(RB):
            for k in range(2):
                dense[r * CB + first_col + k] = g[r * BS:(r + 1) * BS, k * BS:(k + 1) * BS]

    def both_products(z, c):
        @pl.loop(0, 2)
        def _(half):
            products(z, c, half)

    mate_core = 1 - core
    zu, zd, zo = mod4(zz + 1), mod4(zz - 1), mod4(zz + 2)
    both_products(zz, core)
    for h in range(2):
        u, dev = us[h]
        m1[h][0].wait_recv()
        piece = agm.at[h, 0, mod4(u - 1)]
        f_up = send(piece, piece, dev[1])
        m1[h][1].wait_recv()
        piece = agm.at[h, 1, mod4(u + 1)]
        f_dn = send(piece, piece, dev[3])
        m1[h] += [f_up, f_dn]
    to_mate.wait_recv()
    both_products(zz, mate_core)
    up_a.wait_recv()
    fw_a = share(col(zd, core, 0), z_up)
    m_da = share(col(zd, core, 0), mate)
    dn_b.wait_recv()
    fw_b = share(col(zu, core, 1), z_dn)
    m_ub = share(col(zu, core, 1), mate)
    products(zd, core, 0)
    products(zu, core, 1)
    m_da.wait_recv()
    products(zd, mate_core, 0)
    m_ub.wait_recv()
    products(zu, mate_core, 1)

    m2 = [None, None]
    for h in range(2):
        for c in m1[h][2:]:
            c.wait_recv()

        @pl.loop(0, 8)
        def _(j):
            here = pl.ds(pl.multiple_of(j * 512, 512), 512)
            both = 0.0
            for ab in range(2):
                x = agm[h, ab, :, :, here].reshape(64, 512)
                both = both + jnp.dot(sel_m[h, ab], x, preferred_element_type=F32)
            sbm[h, :, :, here] = both.astype(BF16).reshape(4, 16, 512)
        w, dev = ws[h]
        m2[h] = [send(sbm.at[h, mod4(w + d)], rbm.at[h, d], dev[d]) for d in (1, 3, 2)]

    up_b.wait_recv()
    m_db = share(col(zd, core, 1), mate)
    dn_a.wait_recv()
    m_ua = share(col(zu, core, 0), mate)
    products(zd, core, 1)
    products(zu, core, 0)
    m_db.wait_recv()
    products(zd, mate_core, 1)
    m_ua.wait_recv()
    products(zu, mate_core, 0)

    cp_dr.wait()
    rc = lax.broadcasted_iota(I32, (16, NBL), 0)
    cc = lax.broadcasted_iota(I32, (16, NBL), 1)
    my_row = cc == dp * 4 + (rc & 3)

    @pl.loop(0, 8)
    def _(j):
        here = pl.ds(pl.multiple_of(j * 512, 512), 512)
        rows = 0.0
        for quarter in range(4):
            there = pl.ds(pl.multiple_of(quarter * 4096 + j * 512, 512), 512)
            pick = one_hot(my_row & ((rc >> 2) == quarter))
            rows = rows + jnp.dot(pick, drow[:, there], preferred_element_type=F32)
        cur[:, here] = rows


    @pl.loop(0, BS)
    def _(r):
        dwide[pl.ds(r, NBL, stride=BS), :] = drow[:, pl.ds(pl.multiple_of(r * BS, BS), BS)].astype(F32)

    @pl.loop(0, NBL)
    def _(k):
        dblk[k] = dwide[pl.ds(pl.multiple_of(k * BS, BS), BS), :].astype(BF16)

    dblk[NBL] = jnp.zeros((BS, BS), BF16)

    fw_a.wait_recv()
    m_oa = share(col(zo, core, 0), mate)
    fw_b.wait_recv()
    m_ob = share(col(zo, core, 1), mate)
    both_products(zo, core)
    m_oa.wait_recv()
    m_ob.wait_recv()
    both_products(zo, mate_core)
    cp_tab.wait()

    def out_copy(n, slot):
        return pltpu.make_async_copy(
            obuf.at[slot], grad_out.at[:, pl.ds(pl.multiple_of(n * TILE, TILE), TILE)], osem.at[slot])

    def tile(n):
        slot = n % 2
        if n + 1 < TILES:
            w_copy(n + 1, 1 - slot).start()
        w_copy(n, slot).wait()

        @pl.loop(0, CB)
        def _(c):
            for r in range(2):
                k = stab[0, (n * 2 + r) * CB + c]
                cols = pl.ds(pl.multiple_of(c * BS, BS), BS)
                wbuf[slot, r * BS:(r + 1) * BS, cols] += dblk[k]

        if n >= 2:
            out_copy(n - 2, slot).wait()

        obuf[slot] = lax.dot_general(
            cbuf[...], wbuf[slot], (((1,), (1,)), ((), ())), preferred_element_type=F32).astype(BF16)

        out_copy(n, slot).start()

    def fill(h, quarter, chunk, ab):
        for e in range(2):
            o = mod4(ws[h][0] + 2 - 2 * chunk - e)
            dev = o * 4 + quarter if h else quarter * 4 + o
            stage[h, quarter, chunk, ab, e] = dense[stab[1, dev * 4 + h * 2 + ab]]

    s1 = {}
    for ch in range(2):
        for h in range(2):
            u, dev = us[h]
            opp = mod4(u + 2)
            fill(h, opp, ch, 0)
            s1[h, ch, 0] = send(stage.at[h, opp, ch, 0], rx.at[h, ch, 0], dev[1])
            fill(h, opp, ch, 1)
            s1[h, ch, 1] = send(stage.at[h, opp, ch, 1], rx.at[h, ch, 1], dev[3])
        for h in range(2):
            u, dev = us[h]
            qu, qd = mod4(u + 1), mod4(u - 1)
            fill(h, qu, ch, 1)
            s1[h, ch, 2] = send(stage.at[h, qu, ch, 1], ry.at[h, ch, 0, 1], dev[1])
            fill(h, qd, ch, 0)
            s1[h, ch, 3] = send(stage.at[h, qd, ch, 0], ry.at[h, ch, 1, 0], dev[3])
    for ch in range(2):
        for h in range(2):
            u, dev = us[h]
            fill(h, mod4(u + 1), ch, 0)
            fill(h, mod4(u - 1), ch, 1)
            fill(h, u, ch, 0)
            fill(h, u, ch, 1)

    def combine(ch):
        for h in range(2):
            u, dev = us[h]
            for ab, q, d in ((0, mod4(u + 1), 1), (1, mod4(u - 1), 3)):
                s1[h, ch, ab].wait_recv()
                for e in range(2):
                    cb[h, ch, ab, e] = (
                        stage[h, q, ch, ab, e].astype(F32) + rx[h, ch, ab, e].astype(F32)).astype(BF16)
                s1[h, ch, 4 + ab] = send(cb.at[h, ch, ab], ry.at[h, ch, ab, ab], dev[d])

    s2 = [[], []]

    def second(ch):
        for h in range(2):
            u, dev = us[h]
            w, wdev = ws[h]
            for ab, pair in ((0, (4, 3)), (1, (2, 5))):
                for c in pair:
                    s1[h, ch, c].wait_recv()
                for e in range(2):
                    r1[h, ch, e, ab] = (
                        stage[h, u, ch, ab, e].astype(F32) + ry[h, ch, 0, ab, e].astype(F32)
                        + ry[h, ch, 1, ab, e].astype(F32)).astype(BF16)
            for e in range(2):
                d = (2 - 2 * ch - e) % 4
                if d:
                    s2[h].append(send(r1.at[h, ch, e], ry2.at[h, d], wdev[d]))

    tile(0)
    combine(0)
    tile(1)
    combine(1)
    second(0)
    tile(2)
    second(1)
    tile(3)
    for h in range(2):
        w, wdev = ws[h]
        for c in s2[h]:
            c.wait_recv()
        for ab in range(2):
            total = r1[h, 1, 0, ab].astype(F32)
            for d in (1, 2, 3):
                total = total + ry2[h, d, ab].astype(F32)
            gsum[pl.ds((h * 2 + ab) * BS, BS), :] = total * GRAD_SCALE

    g1 = [None, None]
    for h in range(2):
        u, dev = us[h]

        @pl.loop(0, 16)
        def _(j):
            rows = jnp.concatenate([gsum[pl.ds(quarter * 32 + h * 16 + j, 4, stride=BS), :] for quarter in range(4)], axis=0)
            g16[:, pl.ds(pl.multiple_of(h * 2048 + j * BS, BS), BS)] = rows
            agg[h, u, :, pl.ds(pl.multiple_of(j * BS, BS), BS)] = rows.astype(BF16)
        own = agg.at[h, u]
        g1[h] = [send(own, own, dev[d]) for d in (1, 3, 2)]

    def adam(g, m0, v0):
        m = BETA_ONE * m0 + (1.0 - BETA_ONE) * g
        v = BETA_TWO * v0 + (1.0 - BETA_TWO) * g * g
        return m, v

    for h in range(2):
        for c in m2[h]:
            c.wait_recv()
    d1 = [None, None]
    for h in range(2):
        u, dev = us[h]
        w, wdev = ws[h]

        @pl.loop(0, 16)
        def _(j):
            here = pl.ds(pl.multiple_of(h * 2048 + j * BS, BS), BS)
            parts = []
            for hm in range(2):
                got = sbm[hm, ws[hm][0], :, here].astype(F32)
                for d in (1, 2, 3):
                    got = got + rbm[hm, d, :, here].astype(F32)
                parts.append(got)
            m0 = jnp.concatenate([p[0:8] for p in parts], axis=0)
            v0 = jnp.concatenate([p[8:16] for p in parts], axis=0)
            m, v = adam(g16[:, here], m0, v0)
            new = cur[:, here] - LEARN_RATE * (m / CORRECT_ONE) / (jnp.sqrt(v / CORRECT_TWO) + EPSILON)
            gath[h, w, u, :, pl.ds(pl.multiple_of(j * BS, BS), BS)] = new.astype(BF16)
        own = gath.at[h, w, u]
        d1[h] = [send(own, own, dev[d]) for d in (1, 3, 2)]

    g2, d2 = [None, None], [None, None]
    for h in range(2):
        for c in g1[h]:
            c.wait_recv()

        @pl.loop(0, 4)
        def _(j):
            here = pl.ds(pl.multiple_of(j * 512, 512), 512)
            x = agg[h, :, :, here].reshape(64, 512)
            sbg[h, :, :, here] = jnp.dot(sel_g[h], x, preferred_element_type=F32).astype(BF16).reshape(4, 32, 512)
    for h in range(2):
        w, dev = ws[h]
        for c in d1[h]:
            c.wait_recv()
        lo, hi = gath.at[h, w, pl.ds(0, 2)], gath.at[h, w, pl.ds(2, 2)]
        d2[h] = [send(lo, lo, dev[1]), send(hi, hi, dev[3])]
    for h in range(2):
        w, dev = ws[h]
        g2[h] = [send(sbg.at[h, mod4(w + d)], rbg.at[h, d], dev[d]) for d in (1, 3, 2)]
        lo, hi = gath.at[h, w, pl.ds(0, 2)], gath.at[h, w, pl.ds(2, 2)]
        d2[h] += [send(hi, hi, dev[1]), send(lo, lo, dev[3])]
    tile(4)
    for h in range(2):
        w, dev = ws[h]
        d2[h][0].wait_recv()
        piece = gath.at[h, mod4(w - 1), pl.ds(0, 2)]
        f_up = send(piece, piece, dev[1])
        d2[h][1].wait_recv()
        piece = gath.at[h, mod4(w + 1), pl.ds(2, 2)]
        f_dn = send(piece, piece, dev[3])
        d2[h] += [f_up, f_dn]
    tile(5)
    for h in range(2):
        w, dev = ws[h]
        for c in g2[h]:
            c.wait_recv()

        @pl.loop(0, 16)
        def _(j):
            here = pl.ds(pl.multiple_of(j * BS, BS), BS)
            got = sbg[h, w, :, here].astype(F32)
            for d in (1, 2, 3):
                got = got + rbg[h, d, :, here].astype(F32)
            for quarter in range(4):
                lanes = pl.ds(pl.multiple_of(quarter * 4096 + h * 2048 + j * BS, BS), BS)
                m0, v0 = mbuf[:, lanes], vbuf[:, lanes]
                m, v = adam(got[quarter * 8:quarter * 8 + 8], m0, v0)
                mnew[:, lanes] = jnp.where(filled, m, m0)
                vnew[:, lanes] = jnp.where(filled, v, v0)
    out_m = local_copy(mnew, first_out, 6)
    out_v = local_copy(vnew, second_out, 7)
    tile(6)
    outs = []
    for h in range(2):
        for c in d2[h][2:]:
            c.wait_recv()

        @pl.loop(0, 4)
        def _(j):
            x = gath[h, :, :, :, pl.ds(pl.multiple_of(j * 512, 512), 512)].reshape(256, 512)
            y = jnp.dot(sel_d[h], x, preferred_element_type=F32).astype(BF16)
            for quarter in range(4):
                lanes = pl.ds(pl.multiple_of(quarter * 4096 + h * 2048 + j * 512, 512), 512)
                dnew[:, lanes] = y[quarter * 64:(quarter + 1) * 64]
        for quarter in range(4):
            lanes = pl.ds(quarter * 4096 + h * 2048, 2048)
            c = pltpu.make_async_copy(dnew.at[:, lanes], deltas_out.at[:, lanes], dsem.at[h * 4 + quarter])
            c.start()
            outs.append(c)
    for c in sent:
        c.wait_send()
    out_m.wait()
    out_v.wait()
    out_copy(TILES - 2, (TILES - 2) % 2).wait()
    out_copy(TILES - 1, (TILES - 1) % 2).wait()
    for c in outs:
        c.wait()


def local(hidden_act, cotangent, weight, deltas, block_ids, owners, first_moment, second_moment):
    any_spec = pl.BlockSpec(memory_space=pl.ANY)
    vm_spec = pl.BlockSpec(memory_space=pltpu.VMEM)
    V = pltpu.VMEM
    outs = pl.pallas_call(
        kernel,
        out_shape=(
            jax.ShapeDtypeStruct((TOK, FFL), BF16),
            jax.ShapeDtypeStruct((NBL, BS * BS), BF16),
            jax.ShapeDtypeStruct((CAP, BS * BS), F32),
            jax.ShapeDtypeStruct((CAP, BS * BS), F32),
        ),
        in_specs=[any_spec] * 4 + [vm_spec] * 2 + [any_spec] * 2,
        out_specs=(any_spec,) * 4,
        scratch_shapes=[
            V((TOK, D), BF16),
            V((TOK, FFL), BF16),
            V((FFL, TOK), BF16),
            V((RB * CB, BS, BS), BF16),
            V((2, TILE, D), BF16),
            V((NBL, BS * BS), BF16),
            V((NBL * BS, BS), F32),
            V((NBL + 1, BS, BS), BF16),
            V((2, 4, 2, 2, 2, BS, BS), BF16),
            V((2, 2, 2, 2, BS, BS), BF16),
            V((2, 2, 2, 2, 2, BS, BS), BF16),
            V((2, 2, 2, 2, BS, BS), BF16),
            V((2, 2, 2, 2, BS, BS), BF16),
            V((2, 4, 2, BS, BS), BF16),
            V((4 * BS, BS), F32),
            V((2, 2, 4, 16, 4096), BF16),
            V((2, 4, 16, 4096), BF16),
            V((2, 4, 16, 4096), BF16),
            V((2, 4, 16, 2048), BF16),
            V((2, 4, 32, 2048), BF16),
            V((2, 4, 32, 2048), BF16),
            V((2, 4, 4, 16, 2048), BF16),
            V((16, 4096), F32),
            V((16, 4096), F32),
            V((CAP, BS * BS), F32),
            V((CAP, BS * BS), F32),
            V((CAP, BS * BS), F32),
            V((CAP, BS * BS), F32),
            V((NBL, BS * BS), BF16),
            V((2, TOK, TILE), BF16),
            V((8, 512), I32),
            pltpu.SMEM((8, 512), I32),
            V((2, 2, 64, 64), BF16),
            V((2, 128, 64), BF16),
            V((2, 256, 256), BF16),
            pltpu.SemaphoreType.DMA((8,)),
            pltpu.SemaphoreType.DMA((2,)),
            pltpu.SemaphoreType.DMA((2,)),
            pltpu.SemaphoreType.DMA((8,)),
            pltpu.SemaphoreType.DMA((N_REMOTE,)),
            pltpu.SemaphoreType.DMA((N_REMOTE,)),
        ],
        compiler_params=pltpu.CompilerParams(
            collective_id=0, has_side_effects=True, vmem_limit_bytes=60 * 1024 * 1024),
        cost_estimate=pl.CostEstimate(flops=15 * 10**9, bytes_accessed=25 * 10**6, transcendentals=0),
    )(
        cotangent, hidden_act, weight, deltas,
        block_ids.reshape(1, NBL), owners.reshape(1, NBL), first_moment[0], second_moment[0],
    )
    input_grad, new_deltas, new_first, new_second = outs
    return (input_grad, new_deltas, new_first[None], new_second[None])


def solution(mesh):
    in_specs = (
        P("dp", "mp"),
        P("dp", "mp"),
        P("mp", None),
        P("mp", None),
        P("mp"),
        P("mp", None),
        P("mp", "dp", None),
        P("mp", "dp", None),
    )
    out_specs = (P("dp", "mp"), P("mp", None), P("mp", "dp", None), P("mp", "dp", None))
    return jax.shard_map(local, mesh=mesh, in_specs=in_specs, out_specs=out_specs, check_vma=False)
```

```python
import functools
import math

import jax
import jax.numpy as jnp
from jax import lax
from jax.experimental import pallas as pl
from jax.experimental.pallas import tpu as pltpu
from jax.sharding import PartitionSpec as P

D = 4096
BS = 128
TOK = 512
FFL = 1792
RB = 14
CB = 32
NBL = 64
CAP = 8
TILES = 7
TILE = FFL // TILES

BETA_ONE = 0.9
BETA_TWO = 0.95
LEARN_RATE = 0.02
EPSILON = 1e-08
CORRECT_ONE = 1.0 - 0.9**4
CORRECT_TWO = 1.0 - 0.95**4
GRAD_SCALE = 1.0 / math.sqrt(8192.0)

MESH = pl.DeviceIdType.MESH
BF16, F32, I32 = jnp.bfloat16, jnp.float32, jnp.int32
N_REMOTE = 96
VMEM_MAIN = 56 * 1024 * 1024
OUT = pltpu.VMEM


def mod4(v):
    return lax.rem(v + 4, 4)


def kernel(
    cot, hid, weight, deltas, ids_row, own_row, first, second,
    grad_out, gath, mnew, vnew,
    cbuf, hbuf, ht, dense, wbuf, drow, dwide, dblk, stage, rx, ry, cb, r1, ry2, gsum,
    agm, sbm, rbm, agg, sbg, rbg, g16, cur, mbuf, vbuf, tab, stab,
    sel_m, sel_g, lsem, wsem, ssem, rsem,
):
    dp, mp = lax.axis_index("dp"), lax.axis_index("mp")
    xx, yy = dp // 4, lax.rem(dp, 4)
    zz, core = mp // 2, lax.rem(mp, 2)
    x_dev = [(mod4(xx + d) * 4 + yy, mp) for d in range(4)]
    y_dev = [(xx * 4 + mod4(yy + d), mp) for d in range(4)]
    z_up, z_dn = (dp, mod4(zz + 1) * 2 + core), (dp, mod4(zz - 1) * 2 + core)
    mate = (dp, zz * 2 + 1 - core)
    us = ((xx, x_dev), (yy, y_dev))
    ws = ((yy, y_dev), (xx, x_dev))

    def local_copy(src, dst, i):
        c = pltpu.make_async_copy(src, dst, lsem.at[i])
        c.start()
        return c

    def col(z, c, half, width=256):
        return pl.ds(pl.multiple_of((z * 2 + c) * 512 + half * 256, 256), width)

    cp_cot = local_copy(cot, cbuf.at[:, col(zz, core, 0, 512)], 0)
    cp_m = local_copy(first, mbuf, 3)
    cp_v = local_copy(second, vbuf, 4)
    cp_hid = local_copy(hid, hbuf, 1)
    cp_dr = local_copy(deltas, drow, 2)

    def w_copy(n, slot):
        return pltpu.make_async_copy(
            weight.at[pl.ds(pl.multiple_of(n * TILE, TILE), TILE)], wbuf.at[slot], wsem.at[slot])

    w_copy(0, 0).start()

    barrier = pltpu.get_barrier_semaphore()
    for dev in (*x_dev[1:], *y_dev[1:], z_up, z_dn, mate):
        pl.semaphore_signal(barrier, inc=1, device_id=dev, device_id_type=MESH)
    pl.semaphore_wait(barrier, 9)

    sent = []

    def send(src, dst, dev):
        i = len(sent)
        c = pltpu.make_async_remote_copy(
            src_ref=src, dst_ref=dst, send_sem=ssem.at[i], recv_sem=rsem.at[i],
            device_id=dev, device_id_type=MESH)
        c.start()
        sent.append(c)
        return c

    def share(where, dev):
        return send(cbuf.at[:, where], cbuf.at[:, where], dev)

    cp_cot.wait()
    up_a = share(col(zz, core, 0), z_up)
    dn_b = share(col(zz, core, 1), z_dn)
    to_mate = share(col(zz, core, 0, 512), mate)
    up_b = share(col(zz, core, 1), z_up)
    dn_a = share(col(zz, core, 0), z_dn)

    cp_m.wait()
    cp_v.wait()
    m1 = [None, None]
    for h in range(2):
        u, dev = us[h]
        for ab in range(2):
            @pl.loop(0, 8)
            def _(j):
                here = pl.ds(pl.multiple_of(j * 512, 512), 512)
                there = pl.ds(pl.multiple_of(h * 8192 + ab * 4096 + j * 512, 512), 512)
                agm[h, ab, u, :, here] = jnp.concatenate([mbuf[:, there], vbuf[:, there]], axis=0).astype(BF16)
        own = [agm.at[h, ab, u] for ab in range(2)]
        m1[h] = [send(own[0], own[0], dev[1]), send(own[1], own[1], dev[3]),
                 send(own[1], own[1], dev[1]), send(own[0], own[0], dev[3])]

    ri = lax.broadcasted_iota(I32, (NBL, NBL), 0)
    ci = lax.broadcasted_iota(I32, (NBL, NBL), 1)
    eye = ri == ci
    owns = jnp.broadcast_to(own_row[...], (NBL, NBL))
    own_col = jnp.sum(jnp.where(eye, owns, 0), axis=1, keepdims=True)
    ids_col = jnp.sum(jnp.where(eye, jnp.broadcast_to(ids_row[...], (NBL, NBL)), 0), axis=1, keepdims=True)
    slot_col = jnp.sum(jnp.where((own_col == owns) & (ci < ri), 1, 0), axis=1, keepdims=True)
    target_col = own_col * CAP + slot_col
    target_row = jnp.sum(jnp.where(eye, jnp.broadcast_to(target_col, (NBL, NBL)), 0), axis=0, keepdims=True)
    block_at = lax.broadcasted_iota(I32, (NBL, 512), 1)
    number = lax.broadcasted_iota(I32, (NBL, 512), 0)
    inverse = NBL - jnp.max(jnp.where(ids_col == block_at, NBL - number, 0), axis=0, keepdims=True)
    tab[...] = jnp.zeros_like(tab)
    tab[0:1, :] = inverse
    tab[1:2, 0:NBL] = ids_row[...]
    cp_tab = local_copy(tab, stab, 5)

    def one_hot(mask):
        return jnp.where(mask, 1.0, 0.0).astype(BF16)

    mine = lax.broadcasted_iota(I32, (16, NBL), 0)
    filled = jnp.max(jnp.where(target_row == dp * CAP + mine, 1, 0), axis=1, keepdims=True)[0:CAP] > 0
    for h in range(2):
        def dev_mem(v):
            return xx * 4 + v if h else v * 4 + yy

        def dev_dest(v):
            return v * 4 + yy if h else xx * 4 + v

        k = dev_dest(ri >> 4) * 4 + (ri & 3)
        wanted = jnp.sum(jnp.where(ci == k, jnp.broadcast_to(target_row, (NBL, NBL)), 0), axis=1, keepdims=True)
        hit = (wanted == dev_mem(ci >> 4) * CAP + (ci & 7)) & (((ri >> 3) & 1) == ((ci >> 3) & 1))
        for half in range(2):
            sel_m[h, half] = one_hot(hit & (((ri >> 2) & 1) == half))
        k = dev_mem(ci >> 4) * 4 + (ci & 3)
        goes = jnp.sum(jnp.where(ri == k, jnp.broadcast_to(target_col, (NBL, NBL)), 0), axis=0, keepdims=True)
        rg = lax.broadcasted_iota(I32, (128, NBL), 0)
        cg = lax.broadcasted_iota(I32, (128, NBL), 1)
        sel_g[h] = one_hot((goes == dev_dest(rg >> 5) * CAP + (rg & 7)) & (((rg >> 3) & 3) == ((cg >> 2) & 3)))

    cp_hid.wait()

    @pl.loop(0, TILES)
    def _(i):
        rows = pl.ds(pl.multiple_of(i * TILE, TILE), TILE)
        ht[rows, :] = hbuf[:, rows].T

    def products(z, c, half):
        first_col = (z * 2 + c) * 4 + half * 2
        g = jnp.dot(ht[...], cbuf[:, col(z, c, half)], preferred_element_type=F32).astype(BF16)
        for r in range(RB):
            for k in range(2):
                dense[r * CB + first_col + k] = g[r * BS:(r + 1) * BS, k * BS:(k + 1) * BS]

    def both_products(z, c):
        @pl.loop(0, 2)
        def _(half):
            products(z, c, half)

    mate_core = 1 - core
    zu, zd, zo = mod4(zz + 1), mod4(zz - 1), mod4(zz + 2)
    both_products(zz, core)
    for h in range(2):
        u, dev = us[h]
        m1[h][0].wait_recv()
        piece = agm.at[h, 0, mod4(u - 1)]
        f_up = send(piece, piece, dev[1])
        m1[h][1].wait_recv()
        piece = agm.at[h, 1, mod4(u + 1)]
        f_dn = send(piece, piece, dev[3])
        m1[h] += [f_up, f_dn]
    to_mate.wait_recv()
    both_products(zz, mate_core)
    up_a.wait_recv()
    fw_a = share(col(zd, core, 0), z_up)
    m_da = share(col(zd, core, 0), mate)
    dn_b.wait_recv()
    fw_b = share(col(zu, core, 1), z_dn)
    m_ub = share(col(zu, core, 1), mate)
    products(zd, core, 0)
    products(zu, core, 1)
    m_da.wait_recv()
    products(zd, mate_core, 0)
    m_ub.wait_recv()
    products(zu, mate_core, 1)

    m2 = [None, None]
    for h in range(2):
        for c in m1[h][2:]:
            c.wait_recv()

        @pl.loop(0, 8)
        def _(j):
            here = pl.ds(pl.multiple_of(j * 512, 512), 512)
            both = 0.0
            for ab in range(2):
                x = agm[h, ab, :, :, here].reshape(64, 512)
                both = both + jnp.dot(sel_m[h, ab], x, preferred_element_type=F32)
            sbm[h, :, :, here] = both.astype(BF16).reshape(4, 16, 512)
        w, dev = ws[h]
        m2[h] = [send(sbm.at[h, mod4(w + d)], rbm.at[h, d], dev[d]) for d in (1, 3, 2)]

    up_b.wait_recv()
    m_db = share(col(zd, core, 1), mate)
    dn_a.wait_recv()
    m_ua = share(col(zu, core, 0), mate)
    products(zd, core, 1)
    products(zu, core, 0)
    m_db.wait_recv()
    products(zd, mate_core, 1)
    m_ua.wait_recv()
    products(zu, mate_core, 0)

    fw_a.wait_recv()
    m_oa = share(col(zo, core, 0), mate)
    fw_b.wait_recv()
    m_ob = share(col(zo, core, 1), mate)
    both_products(zo, core)
    m_oa.wait_recv()
    m_ob.wait_recv()
    both_products(zo, mate_core)
    cp_tab.wait()

    def tile(n):
        slot = n % 2
        if n + 1 < TILES:
            w_copy(n + 1, 1 - slot).start()
        w_copy(n, slot).wait()

        @pl.loop(0, CB)
        def _(c):
            for r in range(2):
                k = stab[0, (n * 2 + r) * CB + c]
                cols = pl.ds(pl.multiple_of(c * BS, BS), BS)
                wbuf[slot, r * BS:(r + 1) * BS, cols] += dblk[k]

        grad_out[:, pl.ds(n * TILE, TILE)] = lax.dot_general(
            cbuf[...], wbuf[slot], (((1,), (1,)), ((), ())), preferred_element_type=F32).astype(BF16)

    def fill(h, quarter, chunk, ab):
        for e in range(2):
            o = mod4(ws[h][0] + 2 - 2 * chunk - e)
            dev = o * 4 + quarter if h else quarter * 4 + o
            stage[h, quarter, chunk, ab, e] = dense[stab[1, dev * 4 + h * 2 + ab]]

    s1 = {}
    for ch in range(2):
        for h in range(2):
            u, dev = us[h]
            opp = mod4(u + 2)
            fill(h, opp, ch, 0)
            s1[h, ch, 0] = send(stage.at[h, opp, ch, 0], rx.at[h, ch, 0], dev[1])
            fill(h, opp, ch, 1)
            s1[h, ch, 1] = send(stage.at[h, opp, ch, 1], rx.at[h, ch, 1], dev[3])
        for h in range(2):
            u, dev = us[h]
            qu, qd = mod4(u + 1), mod4(u - 1)
            fill(h, qu, ch, 1)
            s1[h, ch, 2] = send(stage.at[h, qu, ch, 1], ry.at[h, ch, 0, 1], dev[1])
            fill(h, qd, ch, 0)
            s1[h, ch, 3] = send(stage.at[h, qd, ch, 0], ry.at[h, ch, 1, 0], dev[3])
    for ch in range(2):
        for h in range(2):
            u, dev = us[h]
            fill(h, mod4(u + 1), ch, 0)
            fill(h, mod4(u - 1), ch, 1)
            fill(h, u, ch, 0)
            fill(h, u, ch, 1)

    def combine(ch):
        for h in range(2):
            u, dev = us[h]
            for ab, q, d in ((0, mod4(u + 1), 1), (1, mod4(u - 1), 3)):
                s1[h, ch, ab].wait_recv()
                for e in range(2):
                    cb[h, ch, ab, e] = (
                        stage[h, q, ch, ab, e].astype(F32) + rx[h, ch, ab, e].astype(F32)).astype(BF16)
                s1[h, ch, 4 + ab] = send(cb.at[h, ch, ab], ry.at[h, ch, ab, ab], dev[d])

    s2 = [[], []]

    def second(ch):
        for h in range(2):
            u, dev = us[h]
            w, wdev = ws[h]
            for ab, pair in ((0, (4, 3)), (1, (2, 5))):
                for c in pair:
                    s1[h, ch, c].wait_recv()
                for e in range(2):
                    r1[h, ch, e, ab] = (
                        stage[h, u, ch, ab, e].astype(F32) + ry[h, ch, 0, ab, e].astype(F32)
                        + ry[h, ch, 1, ab, e].astype(F32)).astype(BF16)
            for e in range(2):
                d = (2 - 2 * ch - e) % 4
                if d:
                    s2[h].append(send(r1.at[h, ch, e], ry2.at[h, d], wdev[d]))

    cp_dr.wait()
    rc = lax.broadcasted_iota(I32, (16, NBL), 0)
    cc = lax.broadcasted_iota(I32, (16, NBL), 1)
    my_row = cc == dp * 4 + (rc & 3)

    @pl.loop(0, 8)
    def _(j):
        here = pl.ds(pl.multiple_of(j * 512, 512), 512)
        rows = 0.0
        for quarter in range(4):
            there = pl.ds(pl.multiple_of(quarter * 4096 + j * 512, 512), 512)
            pick = one_hot(my_row & ((rc >> 2) == quarter))
            rows = rows + jnp.dot(pick, drow[:, there], preferred_element_type=F32)
        cur[:, here] = rows


    @pl.loop(0, BS)
    def _(r):
        dwide[pl.ds(r, NBL, stride=BS), :] = drow[:, pl.ds(pl.multiple_of(r * BS, BS), BS)].astype(F32)

    @pl.loop(0, NBL)
    def _(k):
        dblk[k] = dwide[pl.ds(pl.multiple_of(k * BS, BS), BS), :].astype(BF16)

    dblk[NBL] = jnp.zeros((BS, BS), BF16)

    combine(0)
    tile(0)
    combine(1)
    tile(1)
    second(0)
    second(1)
    tile(2)
    tile(3)
    for h in range(2):
        w, wdev = ws[h]
        for c in s2[h]:
            c.wait_recv()
        for ab in range(2):
            total = r1[h, 1, 0, ab].astype(F32)
            for d in (1, 2, 3):
                total = total + ry2[h, d, ab].astype(F32)
            gsum[pl.ds((h * 2 + ab) * BS, BS), :] = total * GRAD_SCALE

    g1 = [None, None]
    for h in range(2):
        u, dev = us[h]

        @pl.loop(0, 4)
        def _(jj):
            for k in range(4):
                j = jj * 4 + k
                rows = jnp.concatenate(
                    [gsum[pl.ds(quarter * 32 + h * 16 + j, 4, stride=BS), :] for quarter in range(4)], axis=0)
                g16[:, pl.ds(pl.multiple_of(h * 2048 + j * BS, BS), BS)] = rows
                agg[h, u, :, pl.ds(pl.multiple_of(j * BS, BS), BS)] = rows.astype(BF16)
        own = agg.at[h, u]
        g1[h] = [send(own, own, dev[d]) for d in (1, 3, 2)]

    def adam(g, m0, v0):
        m = BETA_ONE * m0 + (1.0 - BETA_ONE) * g
        v = BETA_TWO * v0 + (1.0 - BETA_TWO) * g * g
        return m, v

    for h in range(2):
        for c in m2[h]:
            c.wait_recv()
    d1 = [None, None]
    for h in range(2):
        u, dev = us[h]
        w, wdev = ws[h]

        @pl.loop(0, 4)
        def _(j):
            here = pl.ds(pl.multiple_of(h * 2048 + j * 512, 512), 512)
            parts = []
            for hm in range(2):
                got = sbm[hm, ws[hm][0], :, here].astype(F32)
                for d in (1, 2, 3):
                    got = got + rbm[hm, d, :, here].astype(F32)
                parts.append(got)
            m0 = jnp.concatenate([p[0:8] for p in parts], axis=0)
            v0 = jnp.concatenate([p[8:16] for p in parts], axis=0)
            m, v = adam(g16[:, here], m0, v0)
            new = cur[:, here] - LEARN_RATE * (m / CORRECT_ONE) / (jnp.sqrt(v / CORRECT_TWO) + EPSILON)
            gath[h, w, u, :, pl.ds(pl.multiple_of(j * 512, 512), 512)] = new.astype(BF16)
        own = gath.at[h, w, u]
        d1[h] = [send(own, own, dev[d]) for d in (1, 3, 2)]

    g2, d2 = [None, None], [None, None]
    for h in range(2):
        for c in g1[h]:
            c.wait_recv()

        @pl.loop(0, 4)
        def _(j):
            here = pl.ds(pl.multiple_of(j * 512, 512), 512)
            x = agg[h, :, :, here].reshape(64, 512)
            sbg[h, :, :, here] = jnp.dot(sel_g[h], x, preferred_element_type=F32).astype(BF16).reshape(4, 32, 512)
        w, dev = ws[h]
        g2[h] = [send(sbg.at[h, mod4(w + d)], rbg.at[h, d], dev[d]) for d in (2, 1, 3)]
    for h in range(2):
        w, dev = ws[h]
        for c in d1[h]:
            c.wait_recv()
        lo, hi = gath.at[h, w, pl.ds(0, 2)], gath.at[h, w, pl.ds(2, 2)]
        d2[h] = [send(lo, lo, dev[1]), send(hi, hi, dev[3])]
    for h in range(2):
        w, dev = ws[h]
        lo, hi = gath.at[h, w, pl.ds(0, 2)], gath.at[h, w, pl.ds(2, 2)]
        d2[h] += [send(hi, hi, dev[1]), send(lo, lo, dev[3])]
    tile(4)
    for h in range(2):
        w, dev = ws[h]
        d2[h][0].wait_recv()
        piece = gath.at[h, mod4(w - 1), pl.ds(0, 2)]
        f_up = send(piece, piece, dev[1])
        d2[h][1].wait_recv()
        piece = gath.at[h, mod4(w + 1), pl.ds(2, 2)]
        f_dn = send(piece, piece, dev[3])
        d2[h] += [f_up, f_dn]
    tile(5)
    for h in range(2):
        w, dev = ws[h]
        for c in g2[h]:
            c.wait_recv()

        @pl.loop(0, 4)
        def _(j):
            here = pl.ds(pl.multiple_of(j * 512, 512), 512)
            got = sbg[h, w, :, here].astype(F32)
            for d in (1, 2, 3):
                got = got + rbg[h, d, :, here].astype(F32)
            for quarter in range(4):
                lanes = pl.ds(pl.multiple_of(quarter * 4096 + h * 2048 + j * 512, 512), 512)
                m0, v0 = mbuf[:, lanes], vbuf[:, lanes]
                m, v = adam(got[quarter * 8:quarter * 8 + 8], m0, v0)
                mnew[:, lanes] = jnp.where(filled, m, m0)
                vnew[:, lanes] = jnp.where(filled, v, v0)
    tile(6)
    for h in range(2):
        for c in d2[h][2:]:
            c.wait_recv()
    for c in sent:
        c.wait_send()


def finish(grad, gath, mnew, vnew, grad_out, deltas_out, first_out, second_out, dnew, sel, sem):
    copies = [pltpu.make_async_copy(mnew, first_out, sem.at[0]), pltpu.make_async_copy(vnew, second_out, sem.at[1])]
    for k in range(4):
        rows = pl.ds(k * 128, 128)
        copies.append(pltpu.make_async_copy(grad.at[rows], grad_out.at[rows], sem.at[2 + k]))
    for c in copies:
        c.start()
    rd = lax.broadcasted_iota(I32, (256, 256), 0)
    cd = lax.broadcasted_iota(I32, (256, 256), 1)
    group, mem = cd >> 6, (cd >> 4) & 3
    for h in range(2):
        dev = group * 4 + mem if h else mem * 4 + group
        hit = ((rd & 63) == dev * 4 + (cd & 3)) & ((rd >> 6) == ((cd >> 2) & 3))
        sel[...] = jnp.where(hit, 1.0, 0.0).astype(BF16)

        @pl.loop(0, 4)
        def _(j):
            x = gath[h, :, :, :, pl.ds(pl.multiple_of(j * 512, 512), 512)].reshape(256, 512)
            y = jnp.dot(sel[...], x, preferred_element_type=F32).astype(BF16)
            for quarter in range(4):
                lanes = pl.ds(pl.multiple_of(quarter * 4096 + h * 2048 + j * 512, 512), 512)
                dnew[:, lanes] = y[quarter * 64:(quarter + 1) * 64]
        for quarter in range(4):
            lanes = pl.ds(quarter * 4096 + h * 2048, 2048)
            c = pltpu.make_async_copy(dnew.at[:, lanes], deltas_out.at[:, lanes], sem.at[6 + h * 4 + quarter])
            c.start()
            copies.append(c)
    for c in copies:
        c.wait()


def local(hidden_act, cotangent, weight, deltas, block_ids, owners, first_moment, second_moment):
    any_spec = pl.BlockSpec(memory_space=pl.ANY)
    vm_spec = pl.BlockSpec(memory_space=pltpu.VMEM)
    V = pltpu.VMEM
    outs = pl.pallas_call(
        kernel,
        out_shape=(
            OUT((TOK, FFL), BF16),
            OUT((2, 4, 4, 16, 2048), BF16),
            OUT((CAP, BS * BS), F32),
            OUT((CAP, BS * BS), F32),
        ),
        in_specs=[any_spec] * 4 + [vm_spec] * 2 + [any_spec] * 2,
        out_specs=(vm_spec,) * 4,
        scratch_shapes=[
            V((TOK, D), BF16),
            V((TOK, FFL), BF16),
            V((FFL, TOK), BF16),
            V((RB * CB, BS, BS), BF16),
            V((2, TILE, D), BF16),
            V((NBL, BS * BS), BF16),
            V((NBL * BS, BS), F32),
            V((NBL + 1, BS, BS), BF16),
            V((2, 4, 2, 2, 2, BS, BS), BF16),
            V((2, 2, 2, 2, BS, BS), BF16),
            V((2, 2, 2, 2, 2, BS, BS), BF16),
            V((2, 2, 2, 2, BS, BS), BF16),
            V((2, 2, 2, 2, BS, BS), BF16),
            V((2, 4, 2, BS, BS), BF16),
            V((4 * BS, BS), F32),
            V((2, 2, 4, 16, 4096), BF16),
            V((2, 4, 16, 4096), BF16),
            V((2, 4, 16, 4096), BF16),
            V((2, 4, 16, 2048), BF16),
            V((2, 4, 32, 2048), BF16),
            V((2, 4, 32, 2048), BF16),
            V((16, 4096), F32),
            V((16, 4096), F32),
            V((CAP, BS * BS), F32),
            V((CAP, BS * BS), F32),
            V((8, 512), I32),
            pltpu.SMEM((8, 512), I32),
            V((2, 2, 64, 64), BF16),
            V((2, 128, 64), BF16),
            pltpu.SemaphoreType.DMA((8,)),
            pltpu.SemaphoreType.DMA((2,)),
            pltpu.SemaphoreType.DMA((N_REMOTE,)),
            pltpu.SemaphoreType.DMA((N_REMOTE,)),
        ],
        compiler_params=pltpu.CompilerParams(
            collective_id=0, has_side_effects=True, vmem_limit_bytes=VMEM_MAIN),
        cost_estimate=pl.CostEstimate(flops=15 * 10**9, bytes_accessed=25 * 10**6, transcendentals=0),
    )(
        cotangent, hidden_act, weight, deltas,
        block_ids.reshape(1, NBL), owners.reshape(1, NBL), first_moment[0], second_moment[0],
    )
    input_grad, new_deltas, new_first, new_second = pl.pallas_call(
        finish,
        out_shape=(
            jax.ShapeDtypeStruct((TOK, FFL), BF16),
            jax.ShapeDtypeStruct((NBL, BS * BS), BF16),
            jax.ShapeDtypeStruct((CAP, BS * BS), F32),
            jax.ShapeDtypeStruct((CAP, BS * BS), F32),
        ),
        in_specs=[any_spec, vm_spec, any_spec, any_spec],
        out_specs=(any_spec,) * 4,
        scratch_shapes=[
            V((NBL, BS * BS), BF16),
            V((256, 256), BF16),
            pltpu.SemaphoreType.DMA((14,)),
        ],
        compiler_params=pltpu.CompilerParams(vmem_limit_bytes=16 * 1024 * 1024),
        cost_estimate=pl.CostEstimate(flops=5 * 10**8, bytes_accessed=10**7, transcendentals=0),
    )(*outs)
    return (input_grad, new_deltas, new_first[None], new_second[None])


def solution(mesh):
    in_specs = (
        P("dp", "mp"),
        P("dp", "mp"),
        P("mp", None),
        P("mp", None),
        P("mp"),
        P("mp", None),
        P("mp", "dp", None),
        P("mp", "dp", None),
    )
    out_specs = (P("dp", "mp"), P("mp", None), P("mp", "dp", None), P("mp", "dp", None))
    return jax.shard_map(local, mesh=mesh, in_specs=in_specs, out_specs=out_specs, check_vma=False)
```

```python
import functools
import math

import jax
import jax.numpy as jnp
from jax import lax
from jax.experimental import pallas as pl
from jax.experimental.pallas import tpu as pltpu
from jax.sharding import PartitionSpec as P

D = 4096
BS = 128
TOK = 512
FFL = 1792
RB = 14
CB = 32
NBL = 64
CAP = 8
TILES = 7
TILE = FFL // TILES

BETA_ONE = 0.9
BETA_TWO = 0.95
LEARN_RATE = 0.02
EPSILON = 1e-08
CORRECT_ONE = 1.0 - 0.9**4
CORRECT_TWO = 1.0 - 0.95**4
GRAD_SCALE = 1.0 / math.sqrt(8192.0)

MESH = pl.DeviceIdType.MESH
BF16, F32, I32 = jnp.bfloat16, jnp.float32, jnp.int32
N_REMOTE = 96
VMEM_MAIN = 56 * 1024 * 1024
OUT = pltpu.VMEM


def mod4(v):
    return lax.rem(v + 4, 4)


def kernel(
    cot, hid, weight, deltas, ids_row, own_row, first, second,
    grad_out, gath, mnew, vnew,
    cbuf, hbuf, ht, dense, wbuf, drow, dwide, dblk, stage, rx, ry, cb, r1, ry2, gsum,
    agm, sbm, rbm, agg, sbg, rbg, g16, cur, mbuf, vbuf, tab, stab,
    sel_m, sel_g, lsem, wsem, ssem, rsem,
):
    dp, mp = lax.axis_index("dp"), lax.axis_index("mp")
    xx, yy = dp // 4, lax.rem(dp, 4)
    zz, core = mp // 2, lax.rem(mp, 2)
    x_dev = [(mod4(xx + d) * 4 + yy, mp) for d in range(4)]
    y_dev = [(xx * 4 + mod4(yy + d), mp) for d in range(4)]
    z_up, z_dn = (dp, mod4(zz + 1) * 2 + core), (dp, mod4(zz - 1) * 2 + core)
    mate = (dp, zz * 2 + 1 - core)
    us = ((xx, x_dev), (yy, y_dev))
    ws = ((yy, y_dev), (xx, x_dev))

    def local_copy(src, dst, i):
        c = pltpu.make_async_copy(src, dst, lsem.at[i])
        c.start()
        return c

    def col(z, c, half, width=256):
        return pl.ds(pl.multiple_of((z * 2 + c) * 512 + half * 256, 256), width)

    cp_cot = local_copy(cot, cbuf.at[:, col(zz, core, 0, 512)], 0)
    cp_m = local_copy(first, mbuf, 3)
    cp_v = local_copy(second, vbuf, 4)
    cp_hid = local_copy(hid, hbuf, 1)
    cp_dr = local_copy(deltas, drow, 2)

    def w_copy(n, slot):
        return pltpu.make_async_copy(
            weight.at[pl.ds(pl.multiple_of(n * TILE, TILE), TILE)], wbuf.at[slot], wsem.at[slot])

    barrier = pltpu.get_barrier_semaphore()
    for dev in (*x_dev[1:], *y_dev[1:], z_up, z_dn, mate):
        pl.semaphore_signal(barrier, inc=1, device_id=dev, device_id_type=MESH)
    pl.semaphore_wait(barrier, 9)

    sent = []

    def send(src, dst, dev):
        i = len(sent)
        c = pltpu.make_async_remote_copy(
            src_ref=src, dst_ref=dst, send_sem=ssem.at[i], recv_sem=rsem.at[i],
            device_id=dev, device_id_type=MESH)
        c.start()
        sent.append(c)
        return c

    def share(where, dev):
        return send(cbuf.at[:, where], cbuf.at[:, where], dev)

    cp_cot.wait()
    up_a = share(col(zz, core, 0), z_up)
    dn_b = share(col(zz, core, 1), z_dn)
    to_mate = share(col(zz, core, 0, 512), mate)
    up_b = share(col(zz, core, 1), z_up)
    dn_a = share(col(zz, core, 0), z_dn)

    cp_m.wait()
    cp_v.wait()
    m1 = [None, None]
    for h in range(2):
        u, dev = us[h]
        for ab in range(2):
            @pl.loop(0, 8)
            def _(j):
                here = pl.ds(pl.multiple_of(j * 512, 512), 512)
                there = pl.ds(pl.multiple_of(h * 8192 + ab * 4096 + j * 512, 512), 512)
                agm[h, ab, u, :, here] = jnp.concatenate([mbuf[:, there], vbuf[:, there]], axis=0).astype(BF16)
        own = [agm.at[h, ab, u] for ab in range(2)]
        m1[h] = [send(own[0], own[0], dev[1]), send(own[1], own[1], dev[3]),
                 send(own[1], own[1], dev[1]), send(own[0], own[0], dev[3])]

    ri = lax.broadcasted_iota(I32, (NBL, NBL), 0)
    ci = lax.broadcasted_iota(I32, (NBL, NBL), 1)
    eye = ri == ci
    owns = jnp.broadcast_to(own_row[...], (NBL, NBL))
    own_col = jnp.sum(jnp.where(eye, owns, 0), axis=1, keepdims=True)
    ids_col = jnp.sum(jnp.where(eye, jnp.broadcast_to(ids_row[...], (NBL, NBL)), 0), axis=1, keepdims=True)
    slot_col = jnp.sum(jnp.where((own_col == owns) & (ci < ri), 1, 0), axis=1, keepdims=True)
    target_col = own_col * CAP + slot_col
    target_row = jnp.sum(jnp.where(eye, jnp.broadcast_to(target_col, (NBL, NBL)), 0), axis=0, keepdims=True)
    block_at = lax.broadcasted_iota(I32, (NBL, 512), 1)
    number = lax.broadcasted_iota(I32, (NBL, 512), 0)
    inverse = NBL - jnp.max(jnp.where(ids_col == block_at, NBL - number, 0), axis=0, keepdims=True)
    tab[...] = jnp.zeros_like(tab)
    tab[0:1, :] = inverse
    tab[1:2, 0:NBL] = ids_row[...]
    cp_tab = local_copy(tab, stab, 5)

    def one_hot(mask):
        return jnp.where(mask, 1.0, 0.0).astype(BF16)

    mine = lax.broadcasted_iota(I32, (16, NBL), 0)
    filled = jnp.max(jnp.where(target_row == dp * CAP + mine, 1, 0), axis=1, keepdims=True)[0:CAP] > 0
    for h in range(2):
        def dev_mem(v):
            return xx * 4 + v if h else v * 4 + yy

        def dev_dest(v):
            return v * 4 + yy if h else xx * 4 + v

        k = dev_dest(ri >> 4) * 4 + (ri & 3)
        wanted = jnp.sum(jnp.where(ci == k, jnp.broadcast_to(target_row, (NBL, NBL)), 0), axis=1, keepdims=True)
        hit = (wanted == dev_mem(ci >> 4) * CAP + (ci & 7)) & (((ri >> 3) & 1) == ((ci >> 3) & 1))
        for half in range(2):
            sel_m[h, half] = one_hot(hit & (((ri >> 2) & 1) == half))
        k = dev_mem(ci >> 4) * 4 + (ci & 3)
        goes = jnp.sum(jnp.where(ri == k, jnp.broadcast_to(target_col, (NBL, NBL)), 0), axis=0, keepdims=True)
        rg = lax.broadcasted_iota(I32, (128, NBL), 0)
        cg = lax.broadcasted_iota(I32, (128, NBL), 1)
        sel_g[h] = one_hot((goes == dev_dest(rg >> 5) * CAP + (rg & 7)) & (((rg >> 3) & 3) == ((cg >> 2) & 3)))

    cp_hid.wait()
    for n in range(4):
        w_copy(n, n).start()

    @pl.loop(0, TILES)
    def _(i):
        rows = pl.ds(pl.multiple_of(i * TILE, TILE), TILE)
        ht[rows, :] = hbuf[:, rows].T

    def products(z, c, half):
        first_col = (z * 2 + c) * 4 + half * 2
        g = jnp.dot(ht[...], cbuf[:, col(z, c, half)], preferred_element_type=F32).astype(BF16)
        for r in range(RB):
            for k in range(2):
                dense[r * CB + first_col + k] = g[r * BS:(r + 1) * BS, k * BS:(k + 1) * BS]

    def both_products(z, c):
        @pl.loop(0, 2)
        def _(half):
            products(z, c, half)

    mate_core = 1 - core
    zu, zd, zo = mod4(zz + 1), mod4(zz - 1), mod4(zz + 2)
    both_products(zz, core)
    for h in range(2):
        u, dev = us[h]
        m1[h][0].wait_recv()
        piece = agm.at[h, 0, mod4(u - 1)]
        f_up = send(piece, piece, dev[1])
        m1[h][1].wait_recv()
        piece = agm.at[h, 1, mod4(u + 1)]
        f_dn = send(piece, piece, dev[3])
        m1[h] += [f_up, f_dn]
    to_mate.wait_recv()
    both_products(zz, mate_core)
    cp_dr.wait()
    rc = lax.broadcasted_iota(I32, (16, NBL), 0)
    cc = lax.broadcasted_iota(I32, (16, NBL), 1)
    my_row = cc == dp * 4 + (rc & 3)

    @pl.loop(0, 2)
    def _(j):
        here = pl.ds(pl.multiple_of(j * 2048, 2048), 2048)
        rows = 0.0
        for quarter in range(4):
            there = pl.ds(pl.multiple_of(quarter * 4096 + j * 2048, 2048), 2048)
            pick = one_hot(my_row & ((rc >> 2) == quarter))
            rows = rows + jnp.dot(pick, drow[:, there], preferred_element_type=F32)
        cur[:, here] = rows


    @pl.loop(0, BS // 8)
    def _(rr):
        for k in range(8):
            r = rr * 8 + k
            dwide[pl.ds(r, NBL, stride=BS), :] = drow[:, pl.ds(pl.multiple_of(r * BS, BS), BS)].astype(F32)

    @pl.loop(0, NBL // 8)
    def _(k):
        at = pl.multiple_of(k * 8, 8)
        dblk[pl.ds(at, 8)] = dwide[pl.ds(at * BS, 8 * BS), :].astype(BF16).reshape(8, BS, BS)

    dblk[NBL] = jnp.zeros((BS, BS), BF16)

    def merge(n):
        slot = n % 4
        w_copy(n, slot).wait()

        @pl.loop(0, CB // 8)
        def _(c):
            cols = pl.ds(pl.multiple_of(c * 8 * BS, 8 * BS), 8 * BS)
            for r in range(2):
                row = [dblk[stab[0, (n * 2 + r) * CB + c * 8 + j]] for j in range(8)]
                wbuf[slot, r * BS:(r + 1) * BS, cols] += jnp.concatenate(row, axis=1)

    def multiply(n):
        grad_out[:, pl.ds(n * TILE, TILE)] = lax.dot_general(
            cbuf[...], wbuf[n % 4], (((1,), (1,)), ((), ())), preferred_element_type=F32).astype(BF16)
        if n + 4 < TILES:
            w_copy(n + 4, n % 4).start()

    cp_tab.wait()
    merge(0)
    up_a.wait_recv()
    fw_a = share(col(zd, core, 0), z_up)
    m_da = share(col(zd, core, 0), mate)
    dn_b.wait_recv()
    fw_b = share(col(zu, core, 1), z_dn)
    m_ub = share(col(zu, core, 1), mate)
    products(zd, core, 0)
    products(zu, core, 1)
    m_da.wait_recv()
    products(zd, mate_core, 0)
    m_ub.wait_recv()
    products(zu, mate_core, 1)

    m2 = [None, None]
    for h in range(2):
        for c in m1[h][2:]:
            c.wait_recv()

        @pl.loop(0, 2)
        def _(j):
            here = pl.ds(pl.multiple_of(j * 2048, 2048), 2048)
            both = 0.0
            for ab in range(2):
                x = agm[h, ab, :, :, here].reshape(64, 2048)
                both = both + jnp.dot(sel_m[h, ab], x, preferred_element_type=F32)
            sbm[h, :, :, here] = both.astype(BF16).reshape(4, 16, 2048)
        w, dev = ws[h]
        m2[h] = [send(sbm.at[h, mod4(w + d)], rbm.at[h, d], dev[d]) for d in (1, 3, 2)]

    up_b.wait_recv()
    m_db = share(col(zd, core, 1), mate)
    dn_a.wait_recv()
    m_ua = share(col(zu, core, 0), mate)
    products(zd, core, 1)
    products(zu, core, 0)
    m_db.wait_recv()
    products(zd, mate_core, 1)
    m_ua.wait_recv()
    products(zu, mate_core, 0)

    merge(1)
    merge(2)
    merge(3)
    fw_a.wait_recv()
    m_oa = share(col(zo, core, 0), mate)
    fw_b.wait_recv()
    m_ob = share(col(zo, core, 1), mate)
    both_products(zo, core)
    m_oa.wait_recv()
    m_ob.wait_recv()
    both_products(zo, mate_core)

    def fill(h, quarter, chunk, ab):
        for e in range(2):
            o = mod4(ws[h][0] + 2 - 2 * chunk - e)
            dev = o * 4 + quarter if h else quarter * 4 + o
            stage[h, quarter, chunk, ab, e] = dense[stab[1, dev * 4 + h * 2 + ab]]

    s1 = {}
    for ch in range(2):
        for h in range(2):
            u, dev = us[h]
            opp = mod4(u + 2)
            fill(h, opp, ch, 0)
            s1[h, ch, 0] = send(stage.at[h, opp, ch, 0], rx.at[h, ch, 0], dev[1])
            fill(h, opp, ch, 1)
            s1[h, ch, 1] = send(stage.at[h, opp, ch, 1], rx.at[h, ch, 1], dev[3])
        for h in range(2):
            u, dev = us[h]
            qu, qd = mod4(u + 1), mod4(u - 1)
            fill(h, qu, ch, 1)
            s1[h, ch, 2] = send(stage.at[h, qu, ch, 1], ry.at[h, ch, 0, 1], dev[1])
            fill(h, qd, ch, 0)
            s1[h, ch, 3] = send(stage.at[h, qd, ch, 0], ry.at[h, ch, 1, 0], dev[3])
    for ch in range(2):
        for h in range(2):
            u, dev = us[h]
            fill(h, mod4(u + 1), ch, 0)
            fill(h, mod4(u - 1), ch, 1)
            fill(h, u, ch, 0)
            fill(h, u, ch, 1)

    def combine(ch):
        for h in range(2):
            u, dev = us[h]
            for ab, q, d in ((0, mod4(u + 1), 1), (1, mod4(u - 1), 3)):
                s1[h, ch, ab].wait_recv()
                for e in range(2):
                    cb[h, ch, ab, e] = (
                        stage[h, q, ch, ab, e].astype(F32) + rx[h, ch, ab, e].astype(F32)).astype(BF16)
                s1[h, ch, 4 + ab] = send(cb.at[h, ch, ab], ry.at[h, ch, ab, ab], dev[d])

    s2 = [[], []]

    def second(ch):
        for h in range(2):
            u, dev = us[h]
            w, wdev = ws[h]
            for ab, pair in ((0, (4, 3)), (1, (2, 5))):
                for c in pair:
                    s1[h, ch, c].wait_recv()
                for e in range(2):
                    r1[h, ch, e, ab] = (
                        stage[h, u, ch, ab, e].astype(F32) + ry[h, ch, 0, ab, e].astype(F32)
                        + ry[h, ch, 1, ab, e].astype(F32)).astype(BF16)
            for e in range(2):
                d = (2 - 2 * ch - e) % 4
                if d:
                    s2[h].append(send(r1.at[h, ch, e], ry2.at[h, d], wdev[d]))

    multiply(0)
    multiply(1)
    merge(4)
    combine(0)
    multiply(2)
    merge(5)
    combine(1)
    multiply(3)
    second(0)
    second(1)
    merge(6)
    multiply(4)
    multiply(5)
    for h in range(2):
        w, wdev = ws[h]
        for c in s2[h]:
            c.wait_recv()
        for ab in range(2):
            total = r1[h, 1, 0, ab].astype(F32)
            for d in (1, 2, 3):
                total = total + ry2[h, d, ab].astype(F32)
            gsum[pl.ds((h * 2 + ab) * BS, BS), :] = total * GRAD_SCALE

    g1 = [None, None]
    for h in range(2):
        u, dev = us[h]

        @pl.loop(0, 4)
        def _(jj):
            for k in range(4):
                j = jj * 4 + k
                rows = jnp.concatenate(
                    [gsum[pl.ds(quarter * 32 + h * 16 + j, 4, stride=BS), :] for quarter in range(4)], axis=0)
                g16[:, pl.ds(pl.multiple_of(h * 2048 + j * BS, BS), BS)] = rows
                agg[h, u, :, pl.ds(pl.multiple_of(j * BS, BS), BS)] = rows.astype(BF16)
        own = agg.at[h, u]
        g1[h] = [send(own, own, dev[d]) for d in (1, 3, 2)]

    def adam(g, m0, v0):
        m = BETA_ONE * m0 + (1.0 - BETA_ONE) * g
        v = BETA_TWO * v0 + (1.0 - BETA_TWO) * g * g
        return m, v

    for h in range(2):
        for c in m2[h]:
            c.wait_recv()
    d1 = [None, None]
    for h in range(2):
        u, dev = us[h]
        w, wdev = ws[h]

        @pl.loop(0, 4)
        def _(j):
            here = pl.ds(pl.multiple_of(h * 2048 + j * 512, 512), 512)
            parts = []
            for hm in range(2):
                got = sbm[hm, ws[hm][0], :, here].astype(F32)
                for d in (1, 2, 3):
                    got = got + rbm[hm, d, :, here].astype(F32)
                parts.append(got)
            m0 = jnp.concatenate([p[0:8] for p in parts], axis=0)
            v0 = jnp.concatenate([p[8:16] for p in parts], axis=0)
            m, v = adam(g16[:, here], m0, v0)
            new = cur[:, here] - LEARN_RATE * (m / CORRECT_ONE) / (jnp.sqrt(v / CORRECT_TWO) + EPSILON)
            gath[h, w, u, :, pl.ds(pl.multiple_of(j * 512, 512), 512)] = new.astype(BF16)
        own = gath.at[h, w, u]
        d1[h] = [send(own, own, dev[d]) for d in (1, 3, 2)]

    multiply(6)

    g2, d2 = [None, None], [None, None]
    for h in range(2):
        for c in g1[h]:
            c.wait_recv()

        sbg[h] = jnp.dot(
            sel_g[h], agg[h].reshape(64, 2048), preferred_element_type=F32).astype(BF16).reshape(4, 32, 2048)
        w, dev = ws[h]
        g2[h] = [send(sbg.at[h, mod4(w + d)], rbg.at[h, d], dev[d]) for d in (2, 1, 3)]
    for h in range(2):
        w, dev = ws[h]
        for c in d1[h]:
            c.wait_recv()
        lo, hi = gath.at[h, w, pl.ds(0, 2)], gath.at[h, w, pl.ds(2, 2)]
        d2[h] = [send(lo, lo, dev[1]), send(hi, hi, dev[3])]
    for h in range(2):
        w, dev = ws[h]
        lo, hi = gath.at[h, w, pl.ds(0, 2)], gath.at[h, w, pl.ds(2, 2)]
        d2[h] += [send(hi, hi, dev[1]), send(lo, lo, dev[3])]
    for h in range(2):
        w, dev = ws[h]
        d2[h][0].wait_recv()
        piece = gath.at[h, mod4(w - 1), pl.ds(0, 2)]
        f_up = send(piece, piece, dev[1])
        d2[h][1].wait_recv()
        piece = gath.at[h, mod4(w + 1), pl.ds(2, 2)]
        f_dn = send(piece, piece, dev[3])
        d2[h] += [f_up, f_dn]
    for h in range(2):
        w, dev = ws[h]
        for c in g2[h]:
            c.wait_recv()

        @pl.loop(0, 4)
        def _(j):
            here = pl.ds(pl.multiple_of(j * 512, 512), 512)
            got = sbg[h, w, :, here].astype(F32)
            for d in (1, 2, 3):
                got = got + rbg[h, d, :, here].astype(F32)
            for quarter in range(4):
                lanes = pl.ds(pl.multiple_of(quarter * 4096 + h * 2048 + j * 512, 512), 512)
                m0, v0 = mbuf[:, lanes], vbuf[:, lanes]
                m, v = adam(got[quarter * 8:quarter * 8 + 8], m0, v0)
                mnew[:, lanes] = jnp.where(filled, m, m0)
                vnew[:, lanes] = jnp.where(filled, v, v0)
    for h in range(2):
        for c in d2[h][2:]:
            c.wait_recv()
    for c in sent:
        c.wait_send()


def finish(grad, gath, mnew, vnew, grad_out, deltas_out, first_out, second_out, dnew, sel, sem):
    copies = [pltpu.make_async_copy(mnew, first_out, sem.at[0]), pltpu.make_async_copy(vnew, second_out, sem.at[1])]
    for k in range(4):
        rows = pl.ds(k * 128, 128)
        copies.append(pltpu.make_async_copy(grad.at[rows], grad_out.at[rows], sem.at[2 + k]))
    for c in copies:
        c.start()
    rd = lax.broadcasted_iota(I32, (256, 256), 0)
    cd = lax.broadcasted_iota(I32, (256, 256), 1)
    group, mem = cd >> 6, (cd >> 4) & 3
    for h in range(2):
        dev = group * 4 + mem if h else mem * 4 + group
        hit = ((rd & 63) == dev * 4 + (cd & 3)) & ((rd >> 6) == ((cd >> 2) & 3))
        sel[...] = jnp.where(hit, 1.0, 0.0).astype(BF16)

        y = jnp.dot(sel[...], gath[h].reshape(256, 2048), preferred_element_type=F32).astype(BF16)
        for quarter in range(4):
            dnew[:, pl.ds(quarter * 4096 + h * 2048, 2048)] = y[quarter * 64:(quarter + 1) * 64]
        for quarter in range(4):
            lanes = pl.ds(quarter * 4096 + h * 2048, 2048)
            c = pltpu.make_async_copy(dnew.at[:, lanes], deltas_out.at[:, lanes], sem.at[6 + h * 4 + quarter])
            c.start()
            copies.append(c)
    for c in copies:
        c.wait()


def local(hidden_act, cotangent, weight, deltas, block_ids, owners, first_moment, second_moment):
    any_spec = pl.BlockSpec(memory_space=pl.ANY)
    vm_spec = pl.BlockSpec(memory_space=pltpu.VMEM)
    V = pltpu.VMEM
    outs = pl.pallas_call(
        kernel,
        out_shape=(
            OUT((TOK, FFL), BF16),
            OUT((2, 4, 4, 16, 2048), BF16),
            OUT((CAP, BS * BS), F32),
            OUT((CAP, BS * BS), F32),
        ),
        in_specs=[any_spec] * 4 + [vm_spec] * 2 + [any_spec] * 2,
        out_specs=(vm_spec,) * 4,
        scratch_shapes=[
            V((TOK, D), BF16),
            V((TOK, FFL), BF16),
            V((FFL, TOK), BF16),
            V((RB * CB, BS, BS), BF16),
            V((4, TILE, D), BF16),
            V((NBL, BS * BS), BF16),
            V((NBL * BS, BS), F32),
            V((NBL + 1, BS, BS), BF16),
            V((2, 4, 2, 2, 2, BS, BS), BF16),
            V((2, 2, 2, 2, BS, BS), BF16),
            V((2, 2, 2, 2, 2, BS, BS), BF16),
            V((2, 2, 2, 2, BS, BS), BF16),
            V((2, 2, 2, 2, BS, BS), BF16),
            V((2, 4, 2, BS, BS), BF16),
            V((4 * BS, BS), F32),
            V((2, 2, 4, 16, 4096), BF16),
            V((2, 4, 16, 4096), BF16),
            V((2, 4, 16, 4096), BF16),
            V((2, 4, 16, 2048), BF16),
            V((2, 4, 32, 2048), BF16),
            V((2, 4, 32, 2048), BF16),
            V((16, 4096), F32),
            V((16, 4096), F32),
            V((CAP, BS * BS), F32),
            V((CAP, BS * BS), F32),
            V((8, 512), I32),
            pltpu.SMEM((8, 512), I32),
            V((2, 2, 64, 64), BF16),
            V((2, 128, 64), BF16),
            pltpu.SemaphoreType.DMA((8,)),
            pltpu.SemaphoreType.DMA((4,)),
            pltpu.SemaphoreType.DMA((N_REMOTE,)),
            pltpu.SemaphoreType.DMA((N_REMOTE,)),
        ],
        compiler_params=pltpu.CompilerParams(
            collective_id=0, has_side_effects=True, vmem_limit_bytes=VMEM_MAIN),
        cost_estimate=pl.CostEstimate(flops=15 * 10**9, bytes_accessed=25 * 10**6, transcendentals=0),
    )(
        cotangent, hidden_act, weight, deltas,
        block_ids.reshape(1, NBL), owners.reshape(1, NBL), first_moment[0], second_moment[0],
    )
    input_grad, new_deltas, new_first, new_second = pl.pallas_call(
        finish,
        out_shape=(
            jax.ShapeDtypeStruct((TOK, FFL), BF16),
            jax.ShapeDtypeStruct((NBL, BS * BS), BF16),
            jax.ShapeDtypeStruct((CAP, BS * BS), F32),
            jax.ShapeDtypeStruct((CAP, BS * BS), F32),
        ),
        in_specs=[any_spec, vm_spec, any_spec, any_spec],
        out_specs=(any_spec,) * 4,
        scratch_shapes=[
            V((NBL, BS * BS), BF16),
            V((256, 256), BF16),
            pltpu.SemaphoreType.DMA((14,)),
        ],
        compiler_params=pltpu.CompilerParams(vmem_limit_bytes=16 * 1024 * 1024),
        cost_estimate=pl.CostEstimate(flops=5 * 10**8, bytes_accessed=10**7, transcendentals=0),
    )(*outs)
    return (input_grad, new_deltas, new_first[None], new_second[None])


def solution(mesh):
    in_specs = (
        P("dp", "mp"),
        P("dp", "mp"),
        P("mp", None),
        P("mp", None),
        P("mp"),
        P("mp", None),
        P("mp", "dp", None),
        P("mp", "dp", None),
    )
    out_specs = (P("dp", "mp"), P("mp", None), P("mp", "dp", None), P("mp", "dp", None))
    return jax.shard_map(local, mesh=mesh, in_specs=in_specs, out_specs=out_specs, check_vma=False)
```

```python
import functools
import math

import jax
import jax.numpy as jnp
from jax import lax
from jax.experimental import pallas as pl
from jax.experimental.pallas import tpu as pltpu
from jax.sharding import PartitionSpec as P

D = 4096
BS = 128
TOK = 512
FFL = 1792
RB = 14
CB = 32
NBL = 64
CAP = 8
TILES = 7
TILE = FFL // TILES

BETA_ONE = 0.9
BETA_TWO = 0.95
LEARN_RATE = 0.02
EPSILON = 1e-08
CORRECT_ONE = 1.0 - 0.9**4
CORRECT_TWO = 1.0 - 0.95**4
GRAD_SCALE = 1.0 / math.sqrt(8192.0)

MESH = pl.DeviceIdType.MESH
BF16, F32, I32 = jnp.bfloat16, jnp.float32, jnp.int32
N_REMOTE = 96
VMEM_MAIN = 56 * 1024 * 1024
OUT = pltpu.VMEM


def mod4(v):
    return lax.rem(v + 4, 4)


def kernel(
    cot, hid, weight, deltas, ids_row, own_row, first, second,
    grad_out, gath, mnew, vnew,
    cbuf, hbuf, ht, dense, wbuf, drow, dwide, dblk, stage, rx, ry, cb, r1, ry2, gsum,
    agm, sbm, rbm, agg, sbg, rbg, g16, cur, mbuf, vbuf, tab, stab,
    sel_m, sel_g, lsem, wsem, ssem, rsem,
):
    dp, mp = lax.axis_index("dp"), lax.axis_index("mp")
    xx, yy = dp // 4, lax.rem(dp, 4)
    zz, core = mp // 2, lax.rem(mp, 2)
    x_dev = [(mod4(xx + d) * 4 + yy, mp) for d in range(4)]
    y_dev = [(xx * 4 + mod4(yy + d), mp) for d in range(4)]
    z_up, z_dn = (dp, mod4(zz + 1) * 2 + core), (dp, mod4(zz - 1) * 2 + core)
    mate = (dp, zz * 2 + 1 - core)
    us = ((xx, x_dev), (yy, y_dev))
    ws = ((yy, y_dev), (xx, x_dev))

    def local_copy(src, dst, i):
        c = pltpu.make_async_copy(src, dst, lsem.at[i])
        c.start()
        return c

    def col(z, c, half, width=256):
        return pl.ds(pl.multiple_of((z * 2 + c) * 512 + half * 256, 256), width)

    cp_cot = local_copy(cot, cbuf.at[:, col(zz, core, 0, 512)], 0)
    cp_m = local_copy(first, mbuf, 3)
    cp_v = local_copy(second, vbuf, 4)
    cp_hid = local_copy(hid, hbuf, 1)
    cp_dr = local_copy(deltas, drow, 2)

    def w_copy(n, slot):
        return pltpu.make_async_copy(
            weight.at[pl.ds(pl.multiple_of(n * TILE, TILE), TILE)], wbuf.at[slot], wsem.at[slot])

    barrier = pltpu.get_barrier_semaphore()
    for dev in (*x_dev[1:], *y_dev[1:], z_up, z_dn, mate):
        pl.semaphore_signal(barrier, inc=1, device_id=dev, device_id_type=MESH)
    pl.semaphore_wait(barrier, 9)

    sent = []

    def send(src, dst, dev):
        i = len(sent)
        c = pltpu.make_async_remote_copy(
            src_ref=src, dst_ref=dst, send_sem=ssem.at[i], recv_sem=rsem.at[i],
            device_id=dev, device_id_type=MESH)
        c.start()
        sent.append(c)
        return c

    def share(where, dev):
        return send(cbuf.at[:, where], cbuf.at[:, where], dev)

    cp_cot.wait()
    up_a = share(col(zz, core, 0), z_up)
    dn_b = share(col(zz, core, 1), z_dn)
    to_mate = share(col(zz, core, 0, 512), mate)
    up_b = share(col(zz, core, 1), z_up)
    dn_a = share(col(zz, core, 0), z_dn)

    cp_m.wait()
    cp_v.wait()
    m1 = [None, None]
    for h in range(2):
        u, dev = us[h]
        for ab in range(2):
            @pl.loop(0, 8)
            def _(j):
                here = pl.ds(pl.multiple_of(j * 512, 512), 512)
                there = pl.ds(pl.multiple_of(h * 8192 + ab * 4096 + j * 512, 512), 512)
                agm[h, ab, u, :, here] = jnp.concatenate([mbuf[:, there], vbuf[:, there]], axis=0).astype(BF16)
        own = [agm.at[h, ab, u] for ab in range(2)]
        m1[h] = [send(own[0], own[0], dev[1]), send(own[1], own[1], dev[3]),
                 send(own[1], own[1], dev[1]), send(own[0], own[0], dev[3])]

    ri = lax.broadcasted_iota(I32, (NBL, NBL), 0)
    ci = lax.broadcasted_iota(I32, (NBL, NBL), 1)
    eye = ri == ci
    owns = jnp.broadcast_to(own_row[...], (NBL, NBL))
    own_col = jnp.sum(jnp.where(eye, owns, 0), axis=1, keepdims=True)
    ids_col = jnp.sum(jnp.where(eye, jnp.broadcast_to(ids_row[...], (NBL, NBL)), 0), axis=1, keepdims=True)
    slot_col = jnp.sum(jnp.where((own_col == owns) & (ci < ri), 1, 0), axis=1, keepdims=True)
    target_col = own_col * CAP + slot_col
    target_row = jnp.sum(jnp.where(eye, jnp.broadcast_to(target_col, (NBL, NBL)), 0), axis=0, keepdims=True)
    block_at = lax.broadcasted_iota(I32, (NBL, 512), 1)
    number = lax.broadcasted_iota(I32, (NBL, 512), 0)
    inverse = NBL - jnp.max(jnp.where(ids_col == block_at, NBL - number, 0), axis=0, keepdims=True)
    tab[...] = jnp.zeros_like(tab)
    tab[0:1, :] = inverse
    tab[1:2, 0:NBL] = ids_row[...]
    cp_tab = local_copy(tab, stab, 5)

    def one_hot(mask):
        return jnp.where(mask, 1.0, 0.0).astype(BF16)

    mine = lax.broadcasted_iota(I32, (16, NBL), 0)
    filled = jnp.max(jnp.where(target_row == dp * CAP + mine, 1, 0), axis=1, keepdims=True)[0:CAP] > 0
    for h in range(2):
        def dev_mem(v):
            return xx * 4 + v if h else v * 4 + yy

        def dev_dest(v):
            return v * 4 + yy if h else xx * 4 + v

        k = dev_dest(ri >> 4) * 4 + (ri & 3)
        wanted = jnp.sum(jnp.where(ci == k, jnp.broadcast_to(target_row, (NBL, NBL)), 0), axis=1, keepdims=True)
        hit = (wanted == dev_mem(ci >> 4) * CAP + (ci & 7)) & (((ri >> 3) & 1) == ((ci >> 3) & 1))
        for half in range(2):
            sel_m[h, half] = one_hot(hit & (((ri >> 2) & 1) == half))
        k = dev_mem(ci >> 4) * 4 + (ci & 3)
        goes = jnp.sum(jnp.where(ri == k, jnp.broadcast_to(target_col, (NBL, NBL)), 0), axis=0, keepdims=True)
        rg = lax.broadcasted_iota(I32, (128, NBL), 0)
        cg = lax.broadcasted_iota(I32, (128, NBL), 1)
        sel_g[h] = one_hot((goes == dev_dest(rg >> 5) * CAP + (rg & 7)) & (((rg >> 3) & 3) == ((cg >> 2) & 3)))

    cp_hid.wait()
    for n in range(4):
        w_copy(n, n).start()

    @pl.loop(0, TILES)
    def _(i):
        rows = pl.ds(pl.multiple_of(i * TILE, TILE), TILE)
        ht[rows, :] = hbuf[:, rows].T

    def products(z, c, half):
        first_col = (z * 2 + c) * 4 + half * 2
        g = jnp.dot(ht[...], cbuf[:, col(z, c, half)], preferred_element_type=F32).astype(BF16)
        for r in range(RB):
            for k in range(2):
                dense[r * CB + first_col + k] = g[r * BS:(r + 1) * BS, k * BS:(k + 1) * BS]

    def both_products(z, c):
        @pl.loop(0, 2)
        def _(half):
            products(z, c, half)

    mate_core = 1 - core
    zu, zd, zo = mod4(zz + 1), mod4(zz - 1), mod4(zz + 2)
    both_products(zz, core)
    for h in range(2):
        u, dev = us[h]
        m1[h][0].wait_recv()
        piece = agm.at[h, 0, mod4(u - 1)]
        f_up = send(piece, piece, dev[1])
        m1[h][1].wait_recv()
        piece = agm.at[h, 1, mod4(u + 1)]
        f_dn = send(piece, piece, dev[3])
        m1[h] += [f_up, f_dn]
    to_mate.wait_recv()
    both_products(zz, mate_core)
    cp_dr.wait()
    rc = lax.broadcasted_iota(I32, (16, NBL), 0)
    cc = lax.broadcasted_iota(I32, (16, NBL), 1)
    my_row = cc == dp * 4 + (rc & 3)

    @pl.loop(0, 2)
    def _(j):
        here = pl.ds(pl.multiple_of(j * 2048, 2048), 2048)
        rows = 0.0
        for quarter in range(4):
            there = pl.ds(pl.multiple_of(quarter * 4096 + j * 2048, 2048), 2048)
            pick = one_hot(my_row & ((rc >> 2) == quarter))
            rows = rows + jnp.dot(pick, drow[:, there], preferred_element_type=F32)
        cur[:, here] = rows


    def merge(n):
        slot = n % 4
        w_copy(n, slot).wait()

        @pl.loop(0, CB // 8)
        def _(c):
            cols = pl.ds(pl.multiple_of(c * 8 * BS, 8 * BS), 8 * BS)
            for r in range(2):
                row = [dblk[stab[0, (n * 2 + r) * CB + c * 8 + j]] for j in range(8)]
                wbuf[slot, r * BS:(r + 1) * BS, cols] += jnp.concatenate(row, axis=1)

    def multiply(n):
        grad_out[:, pl.ds(n * TILE, TILE)] = lax.dot_general(
            cbuf[...], wbuf[n % 4], (((1,), (1,)), ((), ())), preferred_element_type=F32).astype(BF16)
        if n + 4 < TILES:
            w_copy(n + 4, n % 4).start()

    up_a.wait_recv()
    fw_a = share(col(zd, core, 0), z_up)
    m_da = share(col(zd, core, 0), mate)
    dn_b.wait_recv()
    fw_b = share(col(zu, core, 1), z_dn)
    m_ub = share(col(zu, core, 1), mate)
    products(zd, core, 0)
    products(zu, core, 1)
    m_da.wait_recv()
    products(zd, mate_core, 0)
    m_ub.wait_recv()
    products(zu, mate_core, 1)

    m2 = [None, None]
    for h in range(2):
        for c in m1[h][2:]:
            c.wait_recv()

        @pl.loop(0, 2)
        def _(j):
            here = pl.ds(pl.multiple_of(j * 2048, 2048), 2048)
            both = 0.0
            for ab in range(2):
                x = agm[h, ab, :, :, here].reshape(64, 2048)
                both = both + jnp.dot(sel_m[h, ab], x, preferred_element_type=F32)
            sbm[h, :, :, here] = both.astype(BF16).reshape(4, 16, 2048)
        w, dev = ws[h]
        m2[h] = [send(sbm.at[h, mod4(w + d)], rbm.at[h, d], dev[d]) for d in (1, 3, 2)]

    up_b.wait_recv()
    m_db = share(col(zd, core, 1), mate)
    dn_a.wait_recv()
    m_ua = share(col(zu, core, 0), mate)
    products(zd, core, 1)
    products(zu, core, 0)
    m_db.wait_recv()
    products(zd, mate_core, 1)
    m_ua.wait_recv()
    products(zu, mate_core, 0)

    cp_tab.wait()
    fw_a.wait_recv()
    m_oa = share(col(zo, core, 0), mate)
    fw_b.wait_recv()
    m_ob = share(col(zo, core, 1), mate)
    both_products(zo, core)
    m_oa.wait_recv()
    m_ob.wait_recv()
    both_products(zo, mate_core)

    def fill(h, quarter, chunk, ab):
        for e in range(2):
            o = mod4(ws[h][0] + 2 - 2 * chunk - e)
            dev = o * 4 + quarter if h else quarter * 4 + o
            stage[h, quarter, chunk, ab, e] = dense[stab[1, dev * 4 + h * 2 + ab]]

    s1 = {}
    for ch in range(2):
        for h in range(2):
            u, dev = us[h]
            opp = mod4(u + 2)
            fill(h, opp, ch, 0)
            s1[h, ch, 0] = send(stage.at[h, opp, ch, 0], rx.at[h, ch, 0], dev[1])
            fill(h, opp, ch, 1)
            s1[h, ch, 1] = send(stage.at[h, opp, ch, 1], rx.at[h, ch, 1], dev[3])
        for h in range(2):
            u, dev = us[h]
            qu, qd = mod4(u + 1), mod4(u - 1)
            fill(h, qu, ch, 1)
            s1[h, ch, 2] = send(stage.at[h, qu, ch, 1], ry.at[h, ch, 0, 1], dev[1])
            fill(h, qd, ch, 0)
            s1[h, ch, 3] = send(stage.at[h, qd, ch, 0], ry.at[h, ch, 1, 0], dev[3])
    for ch in range(2):
        for h in range(2):
            u, dev = us[h]
            fill(h, mod4(u + 1), ch, 0)
            fill(h, mod4(u - 1), ch, 1)
            fill(h, u, ch, 0)
            fill(h, u, ch, 1)

    def combine(ch):
        for h in range(2):
            u, dev = us[h]
            for ab, q, d in ((0, mod4(u + 1), 1), (1, mod4(u - 1), 3)):
                s1[h, ch, ab].wait_recv()
                for e in range(2):
                    cb[h, ch, ab, e] = (
                        stage[h, q, ch, ab, e].astype(F32) + rx[h, ch, ab, e].astype(F32)).astype(BF16)
                s1[h, ch, 4 + ab] = send(cb.at[h, ch, ab], ry.at[h, ch, ab, ab], dev[d])

    s2 = [[], []]

    def second(ch):
        for h in range(2):
            u, dev = us[h]
            w, wdev = ws[h]
            for ab, pair in ((0, (4, 3)), (1, (2, 5))):
                for c in pair:
                    s1[h, ch, c].wait_recv()
                for e in range(2):
                    r1[h, ch, e, ab] = (
                        stage[h, u, ch, ab, e].astype(F32) + ry[h, ch, 0, ab, e].astype(F32)
                        + ry[h, ch, 1, ab, e].astype(F32)).astype(BF16)
            for e in range(2):
                d = (2 - 2 * ch - e) % 4
                if d:
                    s2[h].append(send(r1.at[h, ch, e], ry2.at[h, d], wdev[d]))

    @pl.loop(0, BS // 8)
    def _(rr):
        for k in range(8):
            r = rr * 8 + k
            dwide[pl.ds(r, NBL, stride=BS), :] = drow[:, pl.ds(pl.multiple_of(r * BS, BS), BS)].astype(F32)

    @pl.loop(0, NBL // 8)
    def _(k):
        at = pl.multiple_of(k * 8, 8)
        dblk[pl.ds(at, 8)] = dwide[pl.ds(at * BS, 8 * BS), :].astype(BF16).reshape(8, BS, BS)

    dblk[NBL] = jnp.zeros((BS, BS), BF16)

    combine(0)
    merge(0)
    merge(1)
    multiply(0)
    combine(1)
    merge(2)
    multiply(1)
    second(0)
    second(1)
    merge(3)
    multiply(2)
    multiply(3)
    for h in range(2):
        w, wdev = ws[h]
        for c in s2[h]:
            c.wait_recv()
        for ab in range(2):
            total = r1[h, 1, 0, ab].astype(F32)
            for d in (1, 2, 3):
                total = total + ry2[h, d, ab].astype(F32)
            gsum[pl.ds((h * 2 + ab) * BS, BS), :] = total * GRAD_SCALE

    g1 = [None, None]
    for h in range(2):
        u, dev = us[h]

        @pl.loop(0, 4)
        def _(jj):
            for k in range(4):
                j = jj * 4 + k
                rows = jnp.concatenate(
                    [gsum[pl.ds(quarter * 32 + h * 16 + j, 4, stride=BS), :] for quarter in range(4)], axis=0)
                g16[:, pl.ds(pl.multiple_of(h * 2048 + j * BS, BS), BS)] = rows
                agg[h, u, :, pl.ds(pl.multiple_of(j * BS, BS), BS)] = rows.astype(BF16)
        own = agg.at[h, u]
        g1[h] = [send(own, own, dev[d]) for d in (1, 3, 2)]

    def adam(g, m0, v0):
        m = BETA_ONE * m0 + (1.0 - BETA_ONE) * g
        v = BETA_TWO * v0 + (1.0 - BETA_TWO) * g * g
        return m, v

    for h in range(2):
        for c in m2[h]:
            c.wait_recv()
    d1 = [None, None]
    for h in range(2):
        u, dev = us[h]
        w, wdev = ws[h]

        @pl.loop(0, 4)
        def _(j):
            here = pl.ds(pl.multiple_of(h * 2048 + j * 512, 512), 512)
            parts = []
            for hm in range(2):
                got = sbm[hm, ws[hm][0], :, here].astype(F32)
                for d in (1, 2, 3):
                    got = got + rbm[hm, d, :, here].astype(F32)
                parts.append(got)
            m0 = jnp.concatenate([p[0:8] for p in parts], axis=0)
            v0 = jnp.concatenate([p[8:16] for p in parts], axis=0)
            m, v = adam(g16[:, here], m0, v0)
            new = cur[:, here] - LEARN_RATE * (m / CORRECT_ONE) / (jnp.sqrt(v / CORRECT_TWO) + EPSILON)
            gath[h, w, u, :, pl.ds(pl.multiple_of(j * 512, 512), 512)] = new.astype(BF16)
        own = gath.at[h, w, u]
        d1[h] = [send(own, own, dev[d]) for d in (1, 3, 2)]

    g2, d2 = [None, None], [None, None]
    for h in range(2):
        for c in g1[h]:
            c.wait_recv()

        sbg[h] = jnp.dot(
            sel_g[h], agg[h].reshape(64, 2048), preferred_element_type=F32).astype(BF16).reshape(4, 32, 2048)
        w, dev = ws[h]
        g2[h] = [send(sbg.at[h, mod4(w + d)], rbg.at[h, d], dev[d]) for d in (2, 1, 3)]
    for h in range(2):
        w, dev = ws[h]
        for c in d1[h]:
            c.wait_recv()
        lo, hi = gath.at[h, w, pl.ds(0, 2)], gath.at[h, w, pl.ds(2, 2)]
        d2[h] = [send(lo, lo, dev[1]), send(hi, hi, dev[3])]
    for h in range(2):
        w, dev = ws[h]
        lo, hi = gath.at[h, w, pl.ds(0, 2)], gath.at[h, w, pl.ds(2, 2)]
        d2[h] += [send(hi, hi, dev[1]), send(lo, lo, dev[3])]
    for n in range(4, TILES):
        merge(n)
        multiply(n)
    for h in range(2):
        w, dev = ws[h]
        for c in g2[h]:
            c.wait_recv()

        @pl.loop(0, 4)
        def _(j):
            here = pl.ds(pl.multiple_of(j * 512, 512), 512)
            got = sbg[h, w, :, here].astype(F32)
            for d in (1, 2, 3):
                got = got + rbg[h, d, :, here].astype(F32)
            for quarter in range(4):
                lanes = pl.ds(pl.multiple_of(quarter * 4096 + h * 2048 + j * 512, 512), 512)
                m0, v0 = mbuf[:, lanes], vbuf[:, lanes]
                m, v = adam(got[quarter * 8:quarter * 8 + 8], m0, v0)
                mnew[:, lanes] = jnp.where(filled, m, m0)
                vnew[:, lanes] = jnp.where(filled, v, v0)
    for h in range(2):
        w, dev = ws[h]
        d2[h][0].wait_recv()
        piece = gath.at[h, mod4(w - 1), pl.ds(0, 2)]
        f_up = send(piece, piece, dev[1])
        d2[h][1].wait_recv()
        piece = gath.at[h, mod4(w + 1), pl.ds(2, 2)]
        f_dn = send(piece, piece, dev[3])
        d2[h] += [f_up, f_dn]
    for h in range(2):
        for c in d2[h][2:]:
            c.wait_recv()
    for c in sent:
        c.wait_send()


def finish(grad, gath, mnew, vnew, grad_out, deltas_out, first_out, second_out, dnew, sel, sem):
    copies = [pltpu.make_async_copy(mnew, first_out, sem.at[0]), pltpu.make_async_copy(vnew, second_out, sem.at[1])]
    for k in range(4):
        rows = pl.ds(k * 128, 128)
        copies.append(pltpu.make_async_copy(grad.at[rows], grad_out.at[rows], sem.at[2 + k]))
    for c in copies:
        c.start()
    rd = lax.broadcasted_iota(I32, (256, 256), 0)
    cd = lax.broadcasted_iota(I32, (256, 256), 1)
    group, mem = cd >> 6, (cd >> 4) & 3
    for h in range(2):
        dev = group * 4 + mem if h else mem * 4 + group
        hit = ((rd & 63) == dev * 4 + (cd & 3)) & ((rd >> 6) == ((cd >> 2) & 3))
        sel[...] = jnp.where(hit, 1.0, 0.0).astype(BF16)

        y = jnp.dot(sel[...], gath[h].reshape(256, 2048), preferred_element_type=F32).astype(BF16)
        for quarter in range(4):
            dnew[:, pl.ds(quarter * 4096 + h * 2048, 2048)] = y[quarter * 64:(quarter + 1) * 64]
        for quarter in range(4):
            lanes = pl.ds(quarter * 4096 + h * 2048, 2048)
            c = pltpu.make_async_copy(dnew.at[:, lanes], deltas_out.at[:, lanes], sem.at[6 + h * 4 + quarter])
            c.start()
            copies.append(c)
    for c in copies:
        c.wait()


def local(hidden_act, cotangent, weight, deltas, block_ids, owners, first_moment, second_moment):
    any_spec = pl.BlockSpec(memory_space=pl.ANY)
    vm_spec = pl.BlockSpec(memory_space=pltpu.VMEM)
    V = pltpu.VMEM
    outs = pl.pallas_call(
        kernel,
        out_shape=(
            OUT((TOK, FFL), BF16),
            OUT((2, 4, 4, 16, 2048), BF16),
            OUT((CAP, BS * BS), F32),
            OUT((CAP, BS * BS), F32),
        ),
        in_specs=[any_spec] * 4 + [vm_spec] * 2 + [any_spec] * 2,
        out_specs=(vm_spec,) * 4,
        scratch_shapes=[
            V((TOK, D), BF16),
            V((TOK, FFL), BF16),
            V((FFL, TOK), BF16),
            V((RB * CB, BS, BS), BF16),
            V((4, TILE, D), BF16),
            V((NBL, BS * BS), BF16),
            V((NBL * BS, BS), F32),
            V((NBL + 1, BS, BS), BF16),
            V((2, 4, 2, 2, 2, BS, BS), BF16),
            V((2, 2, 2, 2, BS, BS), BF16),
            V((2, 2, 2, 2, 2, BS, BS), BF16),
            V((2, 2, 2, 2, BS, BS), BF16),
            V((2, 2, 2, 2, BS, BS), BF16),
            V((2, 4, 2, BS, BS), BF16),
            V((4 * BS, BS), F32),
            V((2, 2, 4, 16, 4096), BF16),
            V((2, 4, 16, 4096), BF16),
            V((2, 4, 16, 4096), BF16),
            V((2, 4, 16, 2048), BF16),
            V((2, 4, 32, 2048), BF16),
            V((2, 4, 32, 2048), BF16),
            V((16, 4096), F32),
            V((16, 4096), F32),
            V((CAP, BS * BS), F32),
            V((CAP, BS * BS), F32),
            V((8, 512), I32),
            pltpu.SMEM((8, 512), I32),
            V((2, 2, 64, 64), BF16),
            V((2, 128, 64), BF16),
            pltpu.SemaphoreType.DMA((8,)),
            pltpu.SemaphoreType.DMA((4,)),
            pltpu.SemaphoreType.DMA((N_REMOTE,)),
            pltpu.SemaphoreType.DMA((N_REMOTE,)),
        ],
        compiler_params=pltpu.CompilerParams(
            collective_id=0, has_side_effects=True, vmem_limit_bytes=VMEM_MAIN),
        cost_estimate=pl.CostEstimate(flops=15 * 10**9, bytes_accessed=25 * 10**6, transcendentals=0),
    )(
        cotangent, hidden_act, weight, deltas,
        block_ids.reshape(1, NBL), owners.reshape(1, NBL), first_moment[0], second_moment[0],
    )
    input_grad, new_deltas, new_first, new_second = pl.pallas_call(
        finish,
        out_shape=(
            jax.ShapeDtypeStruct((TOK, FFL), BF16),
            jax.ShapeDtypeStruct((NBL, BS * BS), BF16),
            jax.ShapeDtypeStruct((CAP, BS * BS), F32),
            jax.ShapeDtypeStruct((CAP, BS * BS), F32),
        ),
        in_specs=[any_spec, vm_spec, any_spec, any_spec],
        out_specs=(any_spec,) * 4,
        scratch_shapes=[
            V((NBL, BS * BS), BF16),
            V((256, 256), BF16),
            pltpu.SemaphoreType.DMA((14,)),
        ],
        compiler_params=pltpu.CompilerParams(vmem_limit_bytes=16 * 1024 * 1024),
        cost_estimate=pl.CostEstimate(flops=5 * 10**8, bytes_accessed=10**7, transcendentals=0),
    )(*outs)
    return (input_grad, new_deltas, new_first[None], new_second[None])


def solution(mesh):
    in_specs = (
        P("dp", "mp"),
        P("dp", "mp"),
        P("mp", None),
        P("mp", None),
        P("mp"),
        P("mp", None),
        P("mp", "dp", None),
        P("mp", "dp", None),
    )
    out_specs = (P("dp", "mp"), P("mp", None), P("mp", "dp", None), P("mp", "dp", None))
    return jax.shard_map(local, mesh=mesh, in_specs=in_specs, out_specs=out_specs, check_vma=False)
```

```python
import functools
import math

import jax
import jax.numpy as jnp
from jax import lax
from jax.experimental import pallas as pl
from jax.experimental.pallas import tpu as pltpu
from jax.sharding import PartitionSpec as P

D = 4096
BS = 128
TOK = 512
FFL = 1792
RB = 14
CB = 32
NBL = 64
CAP = 8
TILES = 7
TILE = FFL // TILES

BETA_ONE = 0.9
BETA_TWO = 0.95
LEARN_RATE = 0.02
EPSILON = 1e-08
CORRECT_ONE = 1.0 - 0.9**4
CORRECT_TWO = 1.0 - 0.95**4
GRAD_SCALE = 1.0 / math.sqrt(8192.0)

MESH = pl.DeviceIdType.MESH
BF16, F32, I32 = jnp.bfloat16, jnp.float32, jnp.int32
N_REMOTE = 128
VMEM_MAIN = 56 * 1024 * 1024
OUT = pltpu.VMEM


def mod4(v):
    return lax.rem(v + 4, 4)


def kernel(
    cot, hid, weight, deltas, ids_row, own_row, first, second,
    grad_out, gath, mnew, vnew,
    cbuf, hbuf, ht, dense, wbuf, drow, dwide, dblk, stage, rx, ry, cb, r1, ry2, gsum,
    agm, sbm, rbm, agg, sbg, rbg, rxg, cbg, g16, cur, mbuf, vbuf, tab, stab,
    sel_m, sel_g, lsem, wsem, ssem, rsem,
):
    dp, mp = lax.axis_index("dp"), lax.axis_index("mp")
    xx, yy = dp // 4, lax.rem(dp, 4)
    zz, core = mp // 2, lax.rem(mp, 2)
    x_dev = [(mod4(xx + d) * 4 + yy, mp) for d in range(4)]
    y_dev = [(xx * 4 + mod4(yy + d), mp) for d in range(4)]
    z_up, z_dn = (dp, mod4(zz + 1) * 2 + core), (dp, mod4(zz - 1) * 2 + core)
    mate = (dp, zz * 2 + 1 - core)
    us = ((xx, x_dev), (yy, y_dev))
    ws = ((yy, y_dev), (xx, x_dev))

    def local_copy(src, dst, i):
        c = pltpu.make_async_copy(src, dst, lsem.at[i])
        c.start()
        return c

    def col(z, c, half, width=256):
        return pl.ds(pl.multiple_of((z * 2 + c) * 512 + half * 256, 256), width)

    cp_cot = local_copy(cot, cbuf.at[:, col(zz, core, 0, 512)], 0)
    cp_m = local_copy(first, mbuf, 3)
    cp_v = local_copy(second, vbuf, 4)
    cp_hid = local_copy(hid, hbuf, 1)
    cp_dr = local_copy(deltas, drow, 2)

    def w_copy(n, slot):
        return pltpu.make_async_copy(
            weight.at[pl.ds(pl.multiple_of(n * TILE, TILE), TILE)], wbuf.at[slot], wsem.at[slot])

    barrier = pltpu.get_barrier_semaphore()
    for dev in (*x_dev[1:], *y_dev[1:], z_up, z_dn, mate):
        pl.semaphore_signal(barrier, inc=1, device_id=dev, device_id_type=MESH)
    pl.semaphore_wait(barrier, 9)

    sent = []

    def send(src, dst, dev):
        i = len(sent)
        c = pltpu.make_async_remote_copy(
            src_ref=src, dst_ref=dst, send_sem=ssem.at[i], recv_sem=rsem.at[i],
            device_id=dev, device_id_type=MESH)
        c.start()
        sent.append(c)
        return c

    def share(where, dev):
        return send(cbuf.at[:, where], cbuf.at[:, where], dev)

    cp_cot.wait()
    up_a = share(col(zz, core, 0), z_up)
    dn_b = share(col(zz, core, 1), z_dn)
    to_mate = share(col(zz, core, 0, 512), mate)
    up_b = share(col(zz, core, 1), z_up)
    dn_a = share(col(zz, core, 0), z_dn)

    cp_m.wait()
    cp_v.wait()
    m1 = [None, None]
    for h in range(2):
        u, dev = us[h]
        for ab in range(2):
            @pl.loop(0, 8)
            def _(j):
                here = pl.ds(pl.multiple_of(j * 512, 512), 512)
                there = pl.ds(pl.multiple_of(h * 8192 + ab * 4096 + j * 512, 512), 512)
                agm[h, ab, u, :, here] = jnp.concatenate([mbuf[:, there], vbuf[:, there]], axis=0).astype(BF16)
        own = [agm.at[h, ab, u] for ab in range(2)]
        m1[h] = [send(own[0], own[0], dev[1]), send(own[1], own[1], dev[3]),
                 send(own[1], own[1], dev[1]), send(own[0], own[0], dev[3])]

    ri = lax.broadcasted_iota(I32, (NBL, NBL), 0)
    ci = lax.broadcasted_iota(I32, (NBL, NBL), 1)
    eye = ri == ci
    owns = jnp.broadcast_to(own_row[...], (NBL, NBL))
    own_col = jnp.sum(jnp.where(eye, owns, 0), axis=1, keepdims=True)
    ids_col = jnp.sum(jnp.where(eye, jnp.broadcast_to(ids_row[...], (NBL, NBL)), 0), axis=1, keepdims=True)
    slot_col = jnp.sum(jnp.where((own_col == owns) & (ci < ri), 1, 0), axis=1, keepdims=True)
    target_col = own_col * CAP + slot_col
    target_row = jnp.sum(jnp.where(eye, jnp.broadcast_to(target_col, (NBL, NBL)), 0), axis=0, keepdims=True)
    block_at = lax.broadcasted_iota(I32, (NBL, 512), 1)
    number = lax.broadcasted_iota(I32, (NBL, 512), 0)
    inverse = NBL - jnp.max(jnp.where(ids_col == block_at, NBL - number, 0), axis=0, keepdims=True)
    tab[...] = jnp.zeros_like(tab)
    tab[0:1, :] = inverse
    tab[1:2, 0:NBL] = ids_row[...]
    cp_tab = local_copy(tab, stab, 5)

    def one_hot(mask):
        return jnp.where(mask, 1.0, 0.0).astype(BF16)

    mine = lax.broadcasted_iota(I32, (16, NBL), 0)
    filled = jnp.max(jnp.where(target_row == dp * CAP + mine, 1, 0), axis=1, keepdims=True)[0:CAP] > 0
    for h in range(2):
        def dev_mem(v):
            return xx * 4 + v if h else v * 4 + yy

        def dev_dest(v):
            return v * 4 + yy if h else xx * 4 + v

        k = dev_dest(ri >> 4) * 4 + (ri & 3)
        wanted = jnp.sum(jnp.where(ci == k, jnp.broadcast_to(target_row, (NBL, NBL)), 0), axis=1, keepdims=True)
        hit = (wanted == dev_mem(ci >> 4) * CAP + (ci & 7)) & (((ri >> 3) & 1) == ((ci >> 3) & 1))
        for half in range(2):
            sel_m[h, half] = one_hot(hit & (((ri >> 2) & 1) == half))
        k = dev_mem(ci >> 4) * 4 + (ci & 3)
        goes = jnp.sum(jnp.where(ri == k, jnp.broadcast_to(target_col, (NBL, NBL)), 0), axis=0, keepdims=True)
        rg = lax.broadcasted_iota(I32, (128, NBL), 0)
        cg = lax.broadcasted_iota(I32, (128, NBL), 1)
        sel_g[h] = one_hot((goes == dev_dest(rg >> 5) * CAP + (rg & 7)) & (((rg >> 3) & 3) == ((cg >> 2) & 3)))

    cp_hid.wait()
    for n in range(4):
        w_copy(n, n).start()

    @pl.loop(0, TILES)
    def _(i):
        rows = pl.ds(pl.multiple_of(i * TILE, TILE), TILE)
        ht[rows, :] = hbuf[:, rows].T

    def products(z, c, half):
        first_col = (z * 2 + c) * 4 + half * 2
        g = jnp.dot(ht[...], cbuf[:, col(z, c, half)], preferred_element_type=F32).astype(BF16)
        for r in range(RB):
            for k in range(2):
                dense[r * CB + first_col + k] = g[r * BS:(r + 1) * BS, k * BS:(k + 1) * BS]

    def both_products(z, c):
        @pl.loop(0, 2)
        def _(half):
            products(z, c, half)

    mate_core = 1 - core
    zu, zd, zo = mod4(zz + 1), mod4(zz - 1), mod4(zz + 2)
    both_products(zz, core)
    for h in range(2):
        u, dev = us[h]
        m1[h][0].wait_recv()
        piece = agm.at[h, 0, mod4(u - 1)]
        f_up = send(piece, piece, dev[1])
        m1[h][1].wait_recv()
        piece = agm.at[h, 1, mod4(u + 1)]
        f_dn = send(piece, piece, dev[3])
        m1[h] += [f_up, f_dn]
    to_mate.wait_recv()
    both_products(zz, mate_core)
    cp_dr.wait()
    rc = lax.broadcasted_iota(I32, (16, NBL), 0)
    cc = lax.broadcasted_iota(I32, (16, NBL), 1)
    my_row = cc == dp * 4 + (rc & 3)

    @pl.loop(0, 2)
    def _(j):
        here = pl.ds(pl.multiple_of(j * 2048, 2048), 2048)
        rows = 0.0
        for quarter in range(4):
            there = pl.ds(pl.multiple_of(quarter * 4096 + j * 2048, 2048), 2048)
            pick = one_hot(my_row & ((rc >> 2) == quarter))
            rows = rows + jnp.dot(pick, drow[:, there], preferred_element_type=F32)
        cur[:, here] = rows


    def merge(n):
        slot = n % 4
        w_copy(n, slot).wait()

        @pl.loop(0, CB // 8)
        def _(c):
            cols = pl.ds(pl.multiple_of(c * 8 * BS, 8 * BS), 8 * BS)
            for r in range(2):
                row = [dblk[stab[0, (n * 2 + r) * CB + c * 8 + j]] for j in range(8)]
                wbuf[slot, r * BS:(r + 1) * BS, cols] += jnp.concatenate(row, axis=1)

    def multiply(n):
        grad_out[:, pl.ds(n * TILE, TILE)] = lax.dot_general(
            cbuf[...], wbuf[n % 4], (((1,), (1,)), ((), ())), preferred_element_type=F32).astype(BF16)
        if n + 4 < TILES:
            w_copy(n + 4, n % 4).start()

    up_a.wait_recv()
    fw_a = share(col(zd, core, 0), z_up)
    m_da = share(col(zd, core, 0), mate)
    dn_b.wait_recv()
    fw_b = share(col(zu, core, 1), z_dn)
    m_ub = share(col(zu, core, 1), mate)
    products(zd, core, 0)
    products(zu, core, 1)
    m_da.wait_recv()
    products(zd, mate_core, 0)
    m_ub.wait_recv()
    products(zu, mate_core, 1)

    m2 = [None, None]
    for h in range(2):
        for c in m1[h][2:]:
            c.wait_recv()

        @pl.loop(0, 2)
        def _(j):
            here = pl.ds(pl.multiple_of(j * 2048, 2048), 2048)
            both = 0.0
            for ab in range(2):
                x = agm[h, ab, :, :, here].reshape(64, 2048)
                both = both + jnp.dot(sel_m[h, ab], x, preferred_element_type=F32)
            sbm[h, :, :, here] = both.astype(BF16).reshape(4, 16, 2048)
        w, dev = ws[h]
        m2[h] = [send(sbm.at[h, mod4(w + d)], rbm.at[h, d], dev[d]) for d in (1, 3, 2)]

    up_b.wait_recv()
    m_db = share(col(zd, core, 1), mate)
    dn_a.wait_recv()
    m_ua = share(col(zu, core, 0), mate)
    products(zd, core, 1)
    products(zu, core, 0)
    m_db.wait_recv()
    products(zd, mate_core, 1)
    m_ua.wait_recv()
    products(zu, mate_core, 0)

    cp_tab.wait()
    fw_a.wait_recv()
    m_oa = share(col(zo, core, 0), mate)
    fw_b.wait_recv()
    m_ob = share(col(zo, core, 1), mate)
    both_products(zo, core)
    m_oa.wait_recv()
    m_ob.wait_recv()
    both_products(zo, mate_core)

    def fill(h, quarter, chunk, ab):
        for e in range(2):
            o = mod4(ws[h][0] + 2 - 2 * chunk - e)
            dev = o * 4 + quarter if h else quarter * 4 + o
            stage[h, quarter, chunk, ab, e] = dense[stab[1, dev * 4 + h * 2 + ab]]

    s1 = {}
    for ch in range(2):
        for h in range(2):
            u, dev = us[h]
            opp = mod4(u + 2)
            fill(h, opp, ch, 0)
            s1[h, ch, 0] = send(stage.at[h, opp, ch, 0], rx.at[h, ch, 0], dev[1])
            fill(h, opp, ch, 1)
            s1[h, ch, 1] = send(stage.at[h, opp, ch, 1], rx.at[h, ch, 1], dev[3])
        for h in range(2):
            u, dev = us[h]
            qu, qd = mod4(u + 1), mod4(u - 1)
            fill(h, qu, ch, 1)
            s1[h, ch, 2] = send(stage.at[h, qu, ch, 1], ry.at[h, ch, 0, 1], dev[1])
            fill(h, qd, ch, 0)
            s1[h, ch, 3] = send(stage.at[h, qd, ch, 0], ry.at[h, ch, 1, 0], dev[3])
    for ch in range(2):
        for h in range(2):
            u, dev = us[h]
            fill(h, mod4(u + 1), ch, 0)
            fill(h, mod4(u - 1), ch, 1)
            fill(h, u, ch, 0)
            fill(h, u, ch, 1)

    def combine(ch):
        for h in range(2):
            u, dev = us[h]
            for ab, q, d in ((0, mod4(u + 1), 1), (1, mod4(u - 1), 3)):
                s1[h, ch, ab].wait_recv()
                for e in range(2):
                    cb[h, ch, ab, e] = (
                        stage[h, q, ch, ab, e].astype(F32) + rx[h, ch, ab, e].astype(F32)).astype(BF16)
                s1[h, ch, 4 + ab] = send(cb.at[h, ch, ab], ry.at[h, ch, ab, ab], dev[d])

    s2 = [[], []]

    def second(ch):
        for h in range(2):
            u, dev = us[h]
            w, wdev = ws[h]
            for ab, pair in ((0, (4, 3)), (1, (2, 5))):
                for c in pair:
                    s1[h, ch, c].wait_recv()
                for e in range(2):
                    r1[h, ch, e, ab] = (
                        stage[h, u, ch, ab, e].astype(F32) + ry[h, ch, 0, ab, e].astype(F32)
                        + ry[h, ch, 1, ab, e].astype(F32)).astype(BF16)
            for e in range(2):
                d = (2 - 2 * ch - e) % 4
                if d:
                    s2[h].append(send(r1.at[h, ch, e], ry2.at[h, d], wdev[d]))

    @pl.loop(0, BS // 8)
    def _(rr):
        for k in range(8):
            r = rr * 8 + k
            dwide[pl.ds(r, NBL, stride=BS), :] = drow[:, pl.ds(pl.multiple_of(r * BS, BS), BS)].astype(F32)

    @pl.loop(0, NBL // 8)
    def _(k):
        at = pl.multiple_of(k * 8, 8)
        dblk[pl.ds(at, 8)] = dwide[pl.ds(at * BS, 8 * BS), :].astype(BF16).reshape(8, BS, BS)

    dblk[NBL] = jnp.zeros((BS, BS), BF16)

    combine(0)
    merge(0)
    merge(1)
    multiply(0)
    combine(1)
    merge(2)
    multiply(1)
    second(0)
    second(1)
    merge(3)
    multiply(2)
    multiply(3)
    for h in range(2):
        w, wdev = ws[h]
        for c in s2[h]:
            c.wait_recv()
        for ab in range(2):
            total = r1[h, 1, 0, ab].astype(F32)
            for d in (1, 2, 3):
                total = total + ry2[h, d, ab].astype(F32)
            gsum[pl.ds((h * 2 + ab) * BS, BS), :] = total * GRAD_SCALE

    g1 = [None, None]
    for h in range(2):
        u, dev = us[h]

        @pl.loop(0, 4)
        def _(jj):
            for k in range(4):
                j = jj * 4 + k
                rows = jnp.concatenate(
                    [gsum[pl.ds(quarter * 32 + h * 16 + j, 4, stride=BS), :] for quarter in range(4)], axis=0)
                g16[:, pl.ds(pl.multiple_of(h * 2048 + j * BS, BS), BS)] = rows
                agg[h, u, :, pl.ds(pl.multiple_of(j * BS, BS), BS)] = rows.astype(BF16)
        own = agg.at[h, u]
        g1[h] = [send(own, own, dev[d]) for d in (1, 3, 2)]

    def adam(g, m0, v0):
        m = BETA_ONE * m0 + (1.0 - BETA_ONE) * g
        v = BETA_TWO * v0 + (1.0 - BETA_TWO) * g * g
        return m, v

    for h in range(2):
        for c in m2[h]:
            c.wait_recv()
    d1 = [None, None]
    for h in range(2):
        u, dev = us[h]
        w, wdev = ws[h]

        @pl.loop(0, 4)
        def _(j):
            here = pl.ds(pl.multiple_of(h * 2048 + j * 512, 512), 512)
            parts = []
            for hm in range(2):
                got = sbm[hm, ws[hm][0], :, here].astype(F32)
                for d in (1, 2, 3):
                    got = got + rbm[hm, d, :, here].astype(F32)
                parts.append(got)
            m0 = jnp.concatenate([p[0:8] for p in parts], axis=0)
            v0 = jnp.concatenate([p[8:16] for p in parts], axis=0)
            m, v = adam(g16[:, here], m0, v0)
            new = cur[:, here] - LEARN_RATE * (m / CORRECT_ONE) / (jnp.sqrt(v / CORRECT_TWO) + EPSILON)
            gath[h, w, u, :, pl.ds(pl.multiple_of(j * 512, 512), 512)] = new.astype(BF16)
        own = gath.at[h, w, u]
        d1[h] = [send(own, own, dev[d]) for d in (1, 3, 2)]

    g2, d2 = [None, None], [None, None]
    for h in range(2):
        for c in g1[h]:
            c.wait_recv()

        sbg[h] = jnp.dot(
            sel_g[h], agg[h].reshape(64, 2048), preferred_element_type=F32).astype(BF16).reshape(4, 32, 2048)
        w, dev = ws[h]
        opp, qu, qd = mod4(w + 2), mod4(w + 1), mod4(w - 1)
        lo, hi = pl.ds(0, 16), pl.ds(16, 16)
        g2[h] = [send(sbg.at[h, opp, lo], rxg.at[h, 0], dev[1]), send(sbg.at[h, opp, hi], rxg.at[h, 1], dev[3]),
                 send(sbg.at[h, qu, hi], rbg.at[h, 0, hi], dev[1]), send(sbg.at[h, qd, lo], rbg.at[h, 1, lo], dev[3])]
    for h in range(2):
        w, dev = ws[h]
        for c in d1[h]:
            c.wait_recv()
        lo, hi = gath.at[h, w, pl.ds(0, 2)], gath.at[h, w, pl.ds(2, 2)]
        d2[h] = [send(lo, lo, dev[1]), send(hi, hi, dev[3])]
    for h in range(2):
        w, dev = ws[h]
        lo, hi = gath.at[h, w, pl.ds(0, 2)], gath.at[h, w, pl.ds(2, 2)]
        d2[h] += [send(hi, hi, dev[1]), send(lo, lo, dev[3])]
    merge(4)
    multiply(4)
    for h in range(2):
        w, dev = ws[h]
        for ab, q, d in ((0, mod4(w + 1), 1), (1, mod4(w - 1), 3)):
            g2[h][ab].wait_recv()
            part = slice(ab * 16, ab * 16 + 16)
            cbg[h, ab] = sbg[h, q, part] + rxg[h, ab]
            g2[h].append(send(cbg.at[h, ab], rbg.at[h, ab, part], dev[d]))
    merge(5)
    multiply(5)
    merge(6)
    multiply(6)
    for h in range(2):
        w, dev = ws[h]
        d2[h][0].wait_recv()
        piece = gath.at[h, mod4(w - 1), pl.ds(0, 2)]
        f_up = send(piece, piece, dev[1])
        d2[h][1].wait_recv()
        piece = gath.at[h, mod4(w + 1), pl.ds(2, 2)]
        f_dn = send(piece, piece, dev[3])
        d2[h] += [f_up, f_dn]
    for h in range(2):
        w, dev = ws[h]
        for c in g2[h][2:]:
            c.wait_recv()

        @pl.loop(0, 4)
        def _(j):
            here = pl.ds(pl.multiple_of(j * 512, 512), 512)
            got = sbg[h, w, :, here].astype(F32)
            for d in range(2):
                got = got + rbg[h, d, :, here].astype(F32)
            for quarter in range(4):
                lanes = pl.ds(pl.multiple_of(quarter * 4096 + h * 2048 + j * 512, 512), 512)
                m0, v0 = mbuf[:, lanes], vbuf[:, lanes]
                m, v = adam(got[quarter * 8:quarter * 8 + 8], m0, v0)
                mnew[:, lanes] = jnp.where(filled, m, m0)
                vnew[:, lanes] = jnp.where(filled, v, v0)
    for h in range(2):
        for c in d2[h][2:]:
            c.wait_recv()
    for c in sent:
        c.wait_send()


def finish(grad, gath, mnew, vnew, grad_out, deltas_out, first_out, second_out, dnew, sel, sem):
    copies = [pltpu.make_async_copy(mnew, first_out, sem.at[0]), pltpu.make_async_copy(vnew, second_out, sem.at[1])]
    for k in range(4):
        rows = pl.ds(k * 128, 128)
        copies.append(pltpu.make_async_copy(grad.at[rows], grad_out.at[rows], sem.at[2 + k]))
    for c in copies:
        c.start()
    rd = lax.broadcasted_iota(I32, (256, 256), 0)
    cd = lax.broadcasted_iota(I32, (256, 256), 1)
    group, mem = cd >> 6, (cd >> 4) & 3
    for h in range(2):
        dev = group * 4 + mem if h else mem * 4 + group
        hit = ((rd & 63) == dev * 4 + (cd & 3)) & ((rd >> 6) == ((cd >> 2) & 3))
        sel[...] = jnp.where(hit, 1.0, 0.0).astype(BF16)

        y = jnp.dot(sel[...], gath[h].reshape(256, 2048), preferred_element_type=F32).astype(BF16)
        for quarter in range(4):
            dnew[:, pl.ds(quarter * 4096 + h * 2048, 2048)] = y[quarter * 64:(quarter + 1) * 64]
        for quarter in range(4):
            lanes = pl.ds(quarter * 4096 + h * 2048, 2048)
            c = pltpu.make_async_copy(dnew.at[:, lanes], deltas_out.at[:, lanes], sem.at[6 + h * 4 + quarter])
            c.start()
            copies.append(c)
    for c in copies:
        c.wait()


def local(hidden_act, cotangent, weight, deltas, block_ids, owners, first_moment, second_moment):
    any_spec = pl.BlockSpec(memory_space=pl.ANY)
    vm_spec = pl.BlockSpec(memory_space=pltpu.VMEM)
    V = pltpu.VMEM
    outs = pl.pallas_call(
        kernel,
        out_shape=(
            OUT((TOK, FFL), BF16),
            OUT((2, 4, 4, 16, 2048), BF16),
            OUT((CAP, BS * BS), F32),
            OUT((CAP, BS * BS), F32),
        ),
        in_specs=[any_spec] * 4 + [vm_spec] * 2 + [any_spec] * 2,
        out_specs=(vm_spec,) * 4,
        scratch_shapes=[
            V((TOK, D), BF16),
            V((TOK, FFL), BF16),
            V((FFL, TOK), BF16),
            V((RB * CB, BS, BS), BF16),
            V((4, TILE, D), BF16),
            V((NBL, BS * BS), BF16),
            V((NBL * BS, BS), F32),
            V((NBL + 1, BS, BS), BF16),
            V((2, 4, 2, 2, 2, BS, BS), BF16),
            V((2, 2, 2, 2, BS, BS), BF16),
            V((2, 2, 2, 2, 2, BS, BS), BF16),
            V((2, 2, 2, 2, BS, BS), BF16),
            V((2, 2, 2, 2, BS, BS), BF16),
            V((2, 4, 2, BS, BS), BF16),
            V((4 * BS, BS), F32),
            V((2, 2, 4, 16, 4096), BF16),
            V((2, 4, 16, 4096), BF16),
            V((2, 4, 16, 4096), BF16),
            V((2, 4, 16, 2048), BF16),
            V((2, 4, 32, 2048), BF16),
            V((2, 2, 32, 2048), BF16),
            V((2, 2, 16, 2048), BF16),
            V((2, 2, 16, 2048), BF16),
            V((16, 4096), F32),
            V((16, 4096), F32),
            V((CAP, BS * BS), F32),
            V((CAP, BS * BS), F32),
            V((8, 512), I32),
            pltpu.SMEM((8, 512), I32),
            V((2, 2, 64, 64), BF16),
            V((2, 128, 64), BF16),
            pltpu.SemaphoreType.DMA((8,)),
            pltpu.SemaphoreType.DMA((4,)),
            pltpu.SemaphoreType.DMA((N_REMOTE,)),
            pltpu.SemaphoreType.DMA((N_REMOTE,)),
        ],
        compiler_params=pltpu.CompilerParams(
            collective_id=0, has_side_effects=True, vmem_limit_bytes=VMEM_MAIN),
        cost_estimate=pl.CostEstimate(flops=15 * 10**9, bytes_accessed=25 * 10**6, transcendentals=0),
    )(
        cotangent, hidden_act, weight, deltas,
        block_ids.reshape(1, NBL), owners.reshape(1, NBL), first_moment[0], second_moment[0],
    )
    input_grad, new_deltas, new_first, new_second = pl.pallas_call(
        finish,
        out_shape=(
            jax.ShapeDtypeStruct((TOK, FFL), BF16),
            jax.ShapeDtypeStruct((NBL, BS * BS), BF16),
            jax.ShapeDtypeStruct((CAP, BS * BS), F32),
            jax.ShapeDtypeStruct((CAP, BS * BS), F32),
        ),
        in_specs=[any_spec, vm_spec, any_spec, any_spec],
        out_specs=(any_spec,) * 4,
        scratch_shapes=[
            V((NBL, BS * BS), BF16),
            V((256, 256), BF16),
            pltpu.SemaphoreType.DMA((14,)),
        ],
        compiler_params=pltpu.CompilerParams(vmem_limit_bytes=16 * 1024 * 1024),
        cost_estimate=pl.CostEstimate(flops=5 * 10**8, bytes_accessed=10**7, transcendentals=0),
    )(*outs)
    return (input_grad, new_deltas, new_first[None], new_second[None])


def solution(mesh):
    in_specs = (
        P("dp", "mp"),
        P("dp", "mp"),
        P("mp", None),
        P("mp", None),
        P("mp"),
        P("mp", None),
        P("mp", "dp", None),
        P("mp", "dp", None),
    )
    out_specs = (P("dp", "mp"), P("mp", None), P("mp", "dp", None), P("mp", "dp", None))
    return jax.shard_map(local, mesh=mesh, in_specs=in_specs, out_specs=out_specs, check_vma=False)
```
